32 devices in a mesh: ctx: 8 (over z, x), tp: 4 (over y, core).
Axes of the slice: x: 2, y: 2, z: 4, core: 2. Of those that a mesh axis runs over, the one named last changes fastest.
Arguments:
- tokens_in: bfloat16 [4096, 2048], P('ctx'), may hold values from -6 to 6
- w_query: bfloat16 [2048, 2048], P(None, 'tp'), may hold values from -0.125 to 0.125
- w_key: bfloat16 [2048, 2048], P(None, 'tp'), may hold values from -0.125 to 0.125
- w_value: bfloat16 [2048, 2048], P(None, 'tp'), may hold values from -0.125 to 0.125
- grad_out: bfloat16 [4096, 2048], P('ctx', 'tp'), may hold values from -4 to 4
- trajectory_ends: int32 [4096], P('ctx'), may hold values from 0 to 1, as said below
Outputs:
- grad_tokens: bfloat16 [4096, 2048], P(('ctx', 'tp'))
The draws below stay inside these ranges and needn't reach their ends.
Inputs may be any that keep to these rules, and one draw needn't show every extreme that they name: `trajectory_ends`: 1 marks a token that ends a trajectory, 0 any other token; trajectories may span many blocks.
All inputs are finite; a program needn't handle non-finite values.
Results may differ from the reference program's by a relative error of at most 0.0061.
Values sent between devices are 32-bit elements; how exact they have to be, the bound alone decides.
A program may use at most 128 MiB of HBM per device.

```python
import jax
import jax.numpy as jnp
from jax import lax

D = 2048
HEADS = 16
HD = 128
TOK_DEV = 512
TOKENS = 4096


def draw_trajectory_ends(key, part):
    blocks = TOKENS // TOK_DEV
    key_count, key_place, key_span, key_start = jax.random.split(jax.random.fold_in(key, 17), 4)
    span_blocks = blocks // 2 + jax.random.randint(key_span, (), 0, blocks // 4 + 1)
    first_block = jax.random.randint(key_start, (), 0, blocks - span_blocks + 1)
    block_ids = jnp.arange(blocks)
    inside = (block_ids >= first_block) & (block_ids < first_block + span_blocks)
    counts = jnp.maximum(jax.random.randint(key_count, (blocks, 1), 0, 6) - 2, 0)
    counts = jnp.where(inside[:, None], 0, counts)
    places = jax.random.randint(key_place, (blocks, 3), 0, TOK_DEV)
    active = jnp.arange(3)[None, :] < counts
    column = jnp.arange(TOK_DEV)
    struck = jnp.any((places[:, :, None] == column[None, None, :]) & active[:, :, None], axis=1)
    return struck.astype(jnp.int32).reshape(TOKENS)


def levels(rng, dims, cuts, least, largest):
    factor_of = 1.0
    for dim, shards_of in cuts:
        steps = jax.random.uniform(jax.random.fold_in(jax.random.fold_in(rng, 6), dim), (shards_of,), jnp.float32, least / len(cuts), largest / len(cuts))
        factor_of = factor_of * jnp.repeat(jnp.exp(steps), dims[dim] // shards_of).reshape((-1,) + (1,) * (len(dims) - 1 - dim))
    return factor_of


def bell_draw(stream_key, shape, scale, limit, pieces=(), kind=jnp.bfloat16):
    result = scale * jax.random.normal(stream_key, shape, jnp.float32)
    if pieces:
        result = result * levels(stream_key, shape, pieces, -0.22, 0.18)
    return jnp.clip(result, -limit, limit).astype(kind)


def setup_inputs(seed: int = 0) -> dict:
    key_of = jax.random.split(jax.random.key(seed), 7)
    return {
        "tokens_in": bell_draw(key_of[0], (TOKENS, D), 1.0, 6.0, ((0, 8),)),
        "w_query": bell_draw(key_of[1], (D, HEADS * HD), D ** -0.5, 0.125, ((1, 4),)),
        "w_key": bell_draw(key_of[2], (D, HEADS * HD), D ** -0.5, 0.125, ((1, 4),)),
        "w_value": bell_draw(key_of[3], (D, HEADS * HD), D ** -0.5, 0.125, ((1, 4),)),
        "grad_out": bell_draw(key_of[4], (TOKENS, HEADS * HD), 0.3, 4.0, ((0, 8), (1, 4))),
        "trajectory_ends": draw_trajectory_ends(jax.random.fold_in(key_of[6], 71), 0),
    }


def joined(earlier, later):
    return (later[0] + (1.0 - later[1][0]) * earlier[0], jnp.maximum(earlier[1], later[1]))


def block_masks(end_flags):
    count = end_flags.shape[0]
    before = (jnp.cumsum(end_flags) - end_flags).astype(jnp.int32)
    end_total = jnp.sum(end_flags).astype(jnp.int32)
    opened = (before == 0)
    closed = (end_total - before == 0)
    positions = jnp.arange(count, dtype=jnp.int32)
    pair_mask = (positions[None, :] <= positions[:, None]) & (before[:, None] == before[None, :])
    reset_any = (end_total > 0).astype(jnp.float32).reshape(1)
    return opened, closed, pair_mask, reset_any


def block_summary(queries, key_rows, value_rows, grad_rows, end_flags):
    opened, closed, pair_mask, reset_any = block_masks(end_flags)
    later_vals = value_rows.astype(jnp.float32) * closed[:, None, None].astype(jnp.float32)
    first_grads = grad_rows.astype(jnp.float32) * opened[:, None, None].astype(jnp.float32)
    carry_out = jnp.einsum('shv,shk->hvk', later_vals, key_rows.astype(jnp.float32))
    grads_out = jnp.einsum('thv,thk->hvk', first_grads, queries.astype(jnp.float32))
    return carry_out, grads_out, reset_any


def block_grads(queries, key_rows, value_rows, grad_rows, end_flags, state_in, grads_in):
    opened, closed, pair_mask, reset_any = block_masks(end_flags)
    qf = queries.astype(jnp.float32)
    kf = key_rows.astype(jnp.float32)
    vf = value_rows.astype(jnp.float32)
    gf = grad_rows.astype(jnp.float32)
    scores = jnp.einsum('thv,shv->hts', gf, vf)
    scores = jnp.where(pair_mask[None], scores, 0.0).astype(jnp.bfloat16).astype(jnp.float32)
    attn = jnp.einsum('thk,shk->hts', qf, kf)
    attn = jnp.where(pair_mask[None], attn, 0.0).astype(jnp.bfloat16).astype(jnp.float32)
    state_bf = state_in.astype(jnp.bfloat16).astype(jnp.float32)
    grads_bf = grads_in.astype(jnp.bfloat16).astype(jnp.float32)
    open_f = opened.astype(jnp.float32)[:, None, None]
    close_f = closed.astype(jnp.float32)[:, None, None]
    score_scale = 1.0 / queries.shape[-1]
    dq = jnp.einsum('hts,shk->thk', scores, kf) + open_f * jnp.einsum('thv,hvk->thk', gf, state_bf)
    dk = jnp.einsum('hts,thk->shk', scores, qf) + close_f * jnp.einsum('shv,hvk->shk', vf, grads_bf)
    dv = jnp.einsum('hts,thv->shv', attn, gf) + close_f * jnp.einsum('shk,hvk->shv', kf, grads_bf)
    return ((score_scale * dq).astype(jnp.bfloat16), (score_scale * dk).astype(jnp.bfloat16),
            (score_scale * dv).astype(jnp.bfloat16))


def reference(tokens_in, w_query, w_key, w_value, grad_out, trajectory_ends):
    blocks = TOKENS // TOK_DEV
    shape = (blocks, TOK_DEV, HEADS, HD)
    queries = jnp.dot(tokens_in, w_query, preferred_element_type=jnp.float32).astype(jnp.bfloat16).reshape(shape)
    key_rows = jnp.dot(tokens_in, w_key, preferred_element_type=jnp.float32).astype(jnp.bfloat16).reshape(shape)
    value_rows = jnp.dot(tokens_in, w_value, preferred_element_type=jnp.float32).astype(jnp.bfloat16).reshape(shape)
    grad_rows = grad_out.reshape(shape)
    end_flags = trajectory_ends.reshape(blocks, TOK_DEV)
    carry_out, grads_out, reset_any = jax.vmap(block_summary)(queries, key_rows, value_rows, grad_rows, end_flags)

    def advance(carry, item):
        return joined(carry, item), carry[0]

    empty = (jnp.zeros((HEADS, HD, HD), jnp.float32), jnp.zeros((1,), jnp.float32))
    _, state_in = lax.scan(advance, empty, (carry_out, reset_any))
    _, grads_in = lax.scan(advance, empty, (grads_out, reset_any), reverse=True)
    dq, dk, dv = jax.vmap(block_grads)(queries, key_rows, value_rows, grad_rows, end_flags, state_in, grads_in)
    flat = (TOKENS, HEADS * HD)
    total = jnp.dot(dq.reshape(flat), w_query.T, preferred_element_type=jnp.float32)
    total = total + jnp.dot(dk.reshape(flat), w_key.T, preferred_element_type=jnp.float32)
    total = total + jnp.dot(dv.reshape(flat), w_value.T, preferred_element_type=jnp.float32)
    return total.astype(jnp.bfloat16)
```

```python
import functools

import jax
import jax.numpy as jnp
from jax import lax
from jax.experimental import pallas as pl
from jax.experimental.pallas import tpu as pltpu
from jax.sharding import PartitionSpec as P

HD = 128


def prefix(part, axis, combine, identity):
    count = lax.axis_size(axis)
    place = lax.axis_index(axis)
    ahead = count - 1 - place
    gathered = jax.tree.map(lambda a: lax.all_gather(a, axis), part)
    state = jax.tree.map(lambda a, e: jnp.zeros_like(a) + jnp.asarray(e, a.dtype), part, identity)

    def one(hop, state):
        source = count - 1 - hop
        return combine(
            state, jax.tree.map(lambda a: lax.dynamic_index_in_dim(a, source, 0, False), gathered)
        )

    return lax.fori_loop(0, ahead, one, state)


def joined(earlier, later):
    return (later[0] + (1.0 - later[1][0]) * earlier[0], jnp.maximum(earlier[1], later[1]))


def body(tokens_in, w_query, w_key, w_value, grad_out, trajectory_ends):
    row_count = tokens_in.shape[0]
    head_count = w_query.shape[1] // HD
    shape = (row_count, head_count, HD)
    queries = (
        jnp.dot(tokens_in, w_query, preferred_element_type=jnp.float32)
        .astype(jnp.bfloat16)
        .reshape(shape)
    )
    key_rows = (
        jnp.dot(tokens_in, w_key, preferred_element_type=jnp.float32)
        .astype(jnp.bfloat16)
        .reshape(shape)
    )
    value_rows = (
        jnp.dot(tokens_in, w_value, preferred_element_type=jnp.float32)
        .astype(jnp.bfloat16)
        .reshape(shape)
    )
    grad_rows = grad_out.reshape(shape)
    before = jnp.cumsum(trajectory_ends) - trajectory_ends
    end_total = jnp.sum(trajectory_ends)
    opened = before == 0
    closed = end_total - before == 0
    positions = jnp.arange(row_count, dtype=jnp.int32)
    pair_mask = (positions[None, :] <= positions[:, None]) & (before[:, None] == before[None, :])
    reset_any = (end_total > 0).astype(jnp.float32).reshape(1)
    open_bf = opened.astype(jnp.bfloat16)[:, None, None]
    close_bf = closed.astype(jnp.bfloat16)[:, None, None]
    carry_out = jnp.einsum(
        "shv,shk->hvk", value_rows * close_bf, key_rows, preferred_element_type=jnp.float32
    )
    grads_out = jnp.einsum(
        "thv,thk->hvk", grad_rows * open_bf, queries, preferred_element_type=jnp.float32
    )
    zero_state = jnp.zeros((head_count, HD, HD), jnp.float32)
    zero_flag = jnp.zeros((1,), jnp.float32)
    flag_list = lax.all_gather(reset_any, "ctx", axis=0, tiled=True)
    own_index = lax.axis_index("ctx")
    order = jnp.arange(flag_list.shape[0], dtype=jnp.int32)
    start_from = jnp.max(jnp.where((order < own_index) & (flag_list > 0), order, 0))
    piece = lax.all_gather(carry_out[None], "ctx", axis=0, tiled=True)
    index_list = jnp.arange(piece.shape[0], dtype=jnp.int32)
    weights = ((index_list >= start_from) & (index_list < own_index)).astype(jnp.float32)
    state_in = jnp.sum(weights[:, None, None, None] * piece, axis=0)
    grads_in = prefix((grads_out, reset_any), "ctx", joined, (zero_state, zero_flag))[0]
    scores = jnp.einsum("thv,shv->hts", grad_rows, value_rows, preferred_element_type=jnp.float32)
    scores = jnp.where(pair_mask[None], scores, 0.0).astype(jnp.bfloat16)
    attn = jnp.einsum("thk,shk->hts", queries, key_rows, preferred_element_type=jnp.float32)
    attn = jnp.where(pair_mask[None], attn, 0.0).astype(jnp.bfloat16)
    state_bf = state_in.astype(jnp.bfloat16)
    grads_bf = grads_in.astype(jnp.bfloat16)
    open_f = opened.astype(jnp.float32)[:, None, None]
    close_f = closed.astype(jnp.float32)[:, None, None]
    score_scale = 1.0 / HD
    grad_query = jnp.einsum("hts,shk->thk", scores, key_rows, preferred_element_type=jnp.float32)
    grad_query = grad_query + open_f * jnp.einsum(
        "thv,hvk->thk", grad_rows, state_bf, preferred_element_type=jnp.float32
    )
    grad_key = jnp.einsum("hts,thk->shk", scores, queries, preferred_element_type=jnp.float32)
    grad_key = grad_key + close_f * jnp.einsum(
        "shv,hvk->shk", value_rows, grads_bf, preferred_element_type=jnp.float32
    )
    grad_value = jnp.einsum("hts,thv->shv", attn, grad_rows, preferred_element_type=jnp.float32)
    grad_value = grad_value + close_f * jnp.einsum(
        "shk,hvk->shv", key_rows, grads_bf, preferred_element_type=jnp.float32
    )
    flat = (row_count, head_count * HD)
    grad_query = (score_scale * grad_query).astype(jnp.bfloat16).reshape(flat)
    grad_key = (score_scale * grad_key).astype(jnp.bfloat16).reshape(flat)
    grad_value = (score_scale * grad_value).astype(jnp.bfloat16).reshape(flat)
    dims = (((1,), (1,)), ((), ()))
    total = lax.dot_general(grad_query, w_query, dims, preferred_element_type=jnp.float32)
    total = total + lax.dot_general(grad_key, w_key, dims, preferred_element_type=jnp.float32)
    total = total + lax.dot_general(grad_value, w_value, dims, preferred_element_type=jnp.float32)
    shares = lax.psum_scatter(total, "tp", scatter_dimension=0, tiled=True)
    return shares.astype(jnp.bfloat16)


NN = ((1,), (0,))
NT = ((1,), (1,))
TN = ((0,), (0,))
COLS = 256
BF = jnp.bfloat16
F32 = jnp.float32


def dot(a, b, dims):
    return lax.dot_general(a, b, (dims, ((), ())), preferred_element_type=F32)


def fused(
    nc, nt, tok_hbm, wq_hbm, wk_hbm, wv_hbm, g_hbm, ends_ref, out_ref,
    tok, w, g, qkv, mask, openc, closec, acc, dcat,
    st, fl, xfl, xr, cr, co, bs, br, fin,
    kept, sent, recd, ysent, yrecd,
    load_sem, fl_sem, x_send, x_recv, c_send, c_recv, b_send, b_recv,
    rs_send, rs_recv, y_send, y_recv,
):
    rows, width = tok.shape
    heads = g.shape[0]
    half = heads // 2
    chunks = width // COLS
    share = rows // nt
    ctx = lax.axis_index("ctx")
    tp = lax.axis_index("tp")
    par, pair = ctx % 2, ctx // 2
    pairs = nc // 2
    lo, hi = tp % 2, tp // 2
    mate = ctx + 1 - 2 * par
    core = tp + 1 - 2 * lo
    over = tp + 2 - 4 * hi

    loads = [
        pltpu.make_async_copy(tok_hbm, tok, load_sem.at[0]),
        pltpu.make_async_copy(wk_hbm, w.at[1], load_sem.at[1]),
        pltpu.make_async_copy(wv_hbm, w.at[2], load_sem.at[2]),
        pltpu.make_async_copy(wq_hbm, w.at[0], load_sem.at[3]),
    ]
    g_loads = [
        pltpu.make_async_copy(g_hbm.at[:, pl.ds(h * HD, HD)], g.at[h], load_sem.at[4 + h])
        for h in range(heads)
    ]
    for load in loads + g_loads:
        load.start()
    barrier = pltpu.get_barrier_semaphore()
    pl.semaphore_signal(barrier, inc=1, device_id={"ctx": mate}, device_id_type=pl.DeviceIdType.MESH)
    pl.semaphore_signal(barrier, inc=1, device_id={"tp": core}, device_id_type=pl.DeviceIdType.MESH)
    pl.semaphore_signal(barrier, inc=1, device_id={"tp": over}, device_id_type=pl.DeviceIdType.MESH)

    @pl.when(pair > 0)
    def _():
        pl.semaphore_signal(
            barrier, inc=1, device_id={"ctx": ctx - 2}, device_id_type=pl.DeviceIdType.MESH
        )

    @pl.when(pair < pairs - 1)
    def _():
        pl.semaphore_signal(
            barrier, inc=1, device_id={"ctx": ctx + 2}, device_id_type=pl.DeviceIdType.MESH
        )

    def remote(src, dst, send, recv, device):
        return pltpu.make_async_remote_copy(
            src_ref=src, dst_ref=dst, send_sem=send, recv_sem=recv,
            device_id=device, device_id_type=pl.DeviceIdType.MESH,
        )

    ends_row = jnp.broadcast_to(ends_ref[...].astype(F32), (HD, rows)).astype(BF)
    row_id = lax.broadcasted_iota(jnp.int32, (rows, rows), 0)
    col_id = lax.broadcasted_iota(jnp.int32, (rows, rows), 1)
    below = (row_id < col_id).astype(F32).astype(BF)
    above = (col_id < row_id).astype(F32).astype(BF)
    before_row = dot(ends_row, below, NN)[0:1, :]
    before_col = dot(above, ends_row, NT)
    total = jnp.sum(ends_ref[...].astype(F32), axis=1, keepdims=True)
    openc[...] = (before_col == 0.0).astype(F32)
    closec[...] = (jnp.broadcast_to(total, (rows, HD)) == before_col).astype(F32)
    fl[...] = jnp.broadcast_to((total > 0.0).astype(F32), fl.shape)
    same = before_row == jnp.broadcast_to(before_col[:, 0:1], (rows, rows))
    mask[...] = jnp.where(same & (col_id <= row_id), 1.0, 0.0)

    waits = 3 + jnp.where(pair > 0, 1, 0) + jnp.where(pair < pairs - 1, 1, 0)
    pl.semaphore_wait(barrier, waits)
    flag_copy = remote(fl, xfl, fl_sem.at[0], fl_sem.at[1], {"ctx": mate})
    flag_copy.start()

    block = min(256, rows)
    spans = [(at, at + block) for at in range(0, rows, block)]

    def project(which):
        @pl.loop(0, rows // block)
        def _(step):
            at = pl.ds(pl.multiple_of(step * block, block), block)
            made = dot(tok[at, :], w[which], NN).astype(BF)
            for h in range(heads):
                qkv[which, h, at, :] = made[:, h * HD : (h + 1) * HD]

    def x_copy(d, i):
        return remote(
            st.at[d, (1 - par) * half + i], xr.at[d, i],
            x_send.at[d, i], x_recv.at[d, i], {"ctx": mate},
        )

    loads[0].wait()
    loads[1].wait()
    project(1)
    loads[2].wait()
    project(2)
    for i in range(half):
        h = (1 - par) * half + i
        st[0, h] = dot((qkv[2, h] * closec[...].astype(BF)), qkv[1, h], TN)
        x_copy(0, i).start()
    loads[3].wait()
    project(0)
    for load in g_loads:
        load.wait()
    for i in range(half):
        h = (1 - par) * half + i
        st[1, h] = dot((g[h] * openc[...].astype(BF)), qkv[0, h], TN)
        x_copy(1, i).start()
    for i in range(half):
        h = par * half + i
        st[0, h] = dot((qkv[2, h] * closec[...].astype(BF)), qkv[1, h], TN)
        st[1, h] = dot((g[h] * openc[...].astype(BF)), qkv[0, h], TN)

    def within(h):
        for n, (start, stop) in enumerate(spans):
            at, upto = slice(start, stop), slice(0, stop)
            keep = mask[at, upto]
            scores = (dot(g[h, at, :], qkv[2, h, upto, :], NT) * keep).astype(BF)
            attn = (dot(qkv[0, h, at, :], qkv[1, h, upto, :], NT) * keep).astype(BF)
            acc[0, h, at, :] = dot(scores, qkv[1, h, upto, :], NN)
            dk = dot(scores, qkv[0, h, at, :], TN)
            dv = dot(attn, g[h, at, :], TN)
            if n:
                old = slice(0, start)
                acc[1, h, old, :] += dk[old]
                acc[2, h, old, :] += dv[old]
            acc[1, h, at, :] = dk[at]
            acc[2, h, at, :] = dv[at]

    def within_some(first, last):
        @pl.loop(first, last)
        def _(h):
            within(h)

    def c_copy(d, i):
        return remote(
            co.at[d, i], cr.at[d, i], c_send.at[d, i], c_recv.at[d, i],
            {"ctx": ctx + 2 - 4 * d},
        )

    def b_copy(d, i):
        return remote(bs.at[d, i], br.at[d, i], b_send.at[d, i], b_recv.at[d, i], {"ctx": mate})

    def has_next(d):
        return ((d == 0) & (pair < pairs - 1)) | ((d == 1) & (pair > 0))

    def has_prev(d):
        return ((d == 0) & (pair > 0)) | ((d == 1) & (pair < pairs - 1))

    def carry(d):
        first_here = par == d
        more, begun = has_next(d), has_prev(d)
        own_flag, mate_flag = fl[0:1, :], xfl[0:1, :]
        first_flag = jnp.where(first_here, own_flag, mate_flag)
        second_flag = jnp.where(first_here, mate_flag, own_flag)

        @pl.when(jnp.logical_not(begun))
        def _():
            cr[d] = jnp.zeros(cr.shape[1:], F32)

        for i in range(half):
            x_copy(d, i).wait_recv()
            own, other = st[d, par * half + i], xr[d, i]
            first = jnp.where(first_here, own, other)
            second = jnp.where(first_here, other, own)

            @pl.when(begun)
            def _():
                c_copy(d, i).wait_recv()

            into = cr[d, i]
            inner = first + (1.0 - first_flag) * into

            @pl.when(more)
            def _():
                co[d, i] = second + (1.0 - second_flag) * inner
                c_copy(d, i).start()

            bs[d, i] = jnp.where(first_here, inner, into)
            b_copy(d, i).start()
            fin[d, par * half + i] = jnp.where(first_here, into, inner).astype(BF)

    turn = jnp.where(pair >= pairs // 2, 1, 0)
    cut = half + half // 2
    within_some(0, half)
    flag_copy.wait_recv()
    carry(turn)
    within_some(half, cut)
    carry(1 - turn)
    within_some(cut, heads)

    scale = 1.0 / HD

    def finish(h):
        at = pl.ds(pl.multiple_of(h * HD, HD), HD)
        a_in, b_in = fin[0, h], fin[1, h]
        opened, closed = openc[...], closec[...]
        dq = acc[0, h] + opened * dot(g[h], a_in, NN)
        dk = acc[1, h] + closed * dot(qkv[2, h], b_in, NN)
        dv = acc[2, h] + closed * dot(qkv[1, h], b_in, NT)
        dcat[0, :, at] = (scale * dq).astype(BF)
        dcat[1, :, at] = (scale * dk).astype(BF)
        dcat[2, :, at] = (scale * dv).astype(BF)

    @pl.loop(0, half)
    def _(i):
        finish(par * half + i)

    for i in range(half):
        for d in range(2):
            b_copy(d, i).wait_recv()
            fin[d, (1 - par) * half + i] = br[d, i].astype(BF)
        finish((1 - par) * half + i)

    def rs_copy(part, j):
        return remote(
            sent.at[part, j], recd.at[part, j], rs_send.at[part, j], rs_recv.at[part, j],
            {"tp": core},
        )

    def y_copy(j):
        return remote(ysent.at[j], yrecd.at[j], y_send.at[j], y_recv.at[j], {"tp": over})

    def product(part, j):
        side = jnp.where(part == 0, 1 - hi, hi)
        at = pl.ds(pl.multiple_of(side * 2 * share, 2 * share), 2 * share)
        cols = pl.ds(pl.multiple_of(j * COLS, COLS), COLS)
        made = dot(dcat[0, at, :], w[0, cols, :], NT)
        made = made + dot(dcat[1, at, :], w[1, cols, :], NT)
        made = made + dot(dcat[2, at, :], w[2, cols, :], NT)
        low, high = made[0:share], made[share : 2 * share]
        sent[part, j] = jnp.where(lo == 0, high, low)
        kept[part, j] = jnp.where(lo == 0, low, high)
        rs_copy(part, j).start()

    def pass_on(j):
        rs_copy(0, j).wait_recv()
        ysent[j] = kept[0, j] + recd[0, j]
        y_copy(j).start()

    product(0, 0)

    @pl.loop(1, chunks)
    def _(j):
        product(0, j)
        pass_on(j - 1)

    product(1, 0)
    pass_on(chunks - 1)

    @pl.loop(1, chunks)
    def _(j):
        product(1, j)

    for j in range(chunks):
        rs_copy(1, j).wait_recv()
        y_copy(j).wait_recv()
        out_ref[:, j * COLS : (j + 1) * COLS] = (kept[1, j] + recd[1, j] + yrecd[j]).astype(BF)

    flag_copy.wait_send()
    for d in range(2):
        for i in range(half):
            x_copy(d, i).wait_send()
            b_copy(d, i).wait_send()

        @pl.when(has_next(d))
        def _():
            for i in range(half):
                c_copy(d, i).wait_send()

    @pl.loop(0, chunks)
    def _(j):
        rs_copy(0, j).wait_send()
        rs_copy(1, j).wait_send()
        y_copy(j).wait_send()


def fused_body(nc, nt, tokens_in, w_query, w_key, w_value, grad_out, trajectory_ends):
    rows, width = tokens_in.shape
    inner = w_query.shape[1]
    heads = inner // HD
    half = heads // 2
    share = rows // nt
    chunks = width // COLS
    anywhere = pl.BlockSpec(memory_space=pl.ANY)
    vmem = pl.BlockSpec(memory_space=pltpu.VMEM)
    dma = pltpu.SemaphoreType.DMA
    states = pltpu.VMEM((2, half, HD, HD), F32)
    piece = (chunks, share, COLS)
    return pl.pallas_call(
        functools.partial(fused, nc, nt),
        out_shape=jax.ShapeDtypeStruct((share, width), BF),
        in_specs=[anywhere] * 5 + [vmem],
        out_specs=vmem,
        scratch_shapes=[
            pltpu.VMEM((rows, width), BF),
            pltpu.VMEM((3, width, inner), BF),
            pltpu.VMEM((heads, rows, HD), BF),
            pltpu.VMEM((3, heads, rows, HD), BF),
            pltpu.VMEM((rows, rows), F32),
            pltpu.VMEM((rows, HD), F32),
            pltpu.VMEM((rows, HD), F32),
            pltpu.VMEM((3, heads, rows, HD), F32),
            pltpu.VMEM((3, rows, inner), BF),
            pltpu.VMEM((2, heads, HD, HD), F32),
            pltpu.VMEM((8, HD), F32),
            pltpu.VMEM((8, HD), F32),
            states, states, states, states, states,
            pltpu.VMEM((2, heads, HD, HD), BF),
            pltpu.VMEM((2, *piece), F32),
            pltpu.VMEM((2, *piece), F32),
            pltpu.VMEM((2, *piece), F32),
            pltpu.VMEM(piece, F32),
            pltpu.VMEM(piece, F32),
            dma((4 + heads,)),
            dma((2,)),
            dma((2, half)), dma((2, half)),
            dma((2, half)), dma((2, half)),
            dma((2, half)), dma((2, half)),
            dma((2, chunks)), dma((2, chunks)),
            dma((chunks,)), dma((chunks,)),
        ],
        compiler_params=pltpu.CompilerParams(
            collective_id=0, has_side_effects=True, vmem_limit_bytes=48 * 2**20
        ),
    )(tokens_in, w_query, w_key, w_value, grad_out, trajectory_ends.reshape(1, rows))


def solution(mesh):
    nc, nt = mesh.shape["ctx"], mesh.shape["tp"]

    def local(tokens_in, w_query, w_key, w_value, grad_out, trajectory_ends):
        rows, width = tokens_in.shape
        heads = w_query.shape[1] // HD
        fits = nt == 4 and nc % 2 == 0 and heads % 2 == 0 and rows <= 512
        fits = fits and width % COLS == 0 and rows % 256 == 0
        call = functools.partial(fused_body, nc, nt) if fits else body
        return call(tokens_in, w_query, w_key, w_value, grad_out, trajectory_ends)

    return jax.shard_map(
        local,
        mesh=mesh,
        in_specs=(
            P("ctx", None),
            P(None, "tp"),
            P(None, "tp"),
            P(None, "tp"),
            P("ctx", "tp"),
            P("ctx"),
        ),
        out_specs=P(("ctx", "tp"), None),
        check_vma=False,
    )
```

```python
import functools

import jax
import jax.numpy as jnp
from jax import lax
from jax.experimental import pallas as pl
from jax.experimental.pallas import tpu as pltpu
from jax.sharding import PartitionSpec as P

HD = 128


def prefix(part, axis, combine, identity):
    count = lax.axis_size(axis)
    place = lax.axis_index(axis)
    ahead = count - 1 - place
    gathered = jax.tree.map(lambda a: lax.all_gather(a, axis), part)
    state = jax.tree.map(lambda a, e: jnp.zeros_like(a) + jnp.asarray(e, a.dtype), part, identity)

    def one(hop, state):
        source = count - 1 - hop
        return combine(
            state, jax.tree.map(lambda a: lax.dynamic_index_in_dim(a, source, 0, False), gathered)
        )

    return lax.fori_loop(0, ahead, one, state)


def joined(earlier, later):
    return (later[0] + (1.0 - later[1][0]) * earlier[0], jnp.maximum(earlier[1], later[1]))


def body(tokens_in, w_query, w_key, w_value, grad_out, trajectory_ends):
    row_count = tokens_in.shape[0]
    head_count = w_query.shape[1] // HD
    shape = (row_count, head_count, HD)
    queries = (
        jnp.dot(tokens_in, w_query, preferred_element_type=jnp.float32)
        .astype(jnp.bfloat16)
        .reshape(shape)
    )
    key_rows = (
        jnp.dot(tokens_in, w_key, preferred_element_type=jnp.float32)
        .astype(jnp.bfloat16)
        .reshape(shape)
    )
    value_rows = (
        jnp.dot(tokens_in, w_value, preferred_element_type=jnp.float32)
        .astype(jnp.bfloat16)
        .reshape(shape)
    )
    grad_rows = grad_out.reshape(shape)
    before = jnp.cumsum(trajectory_ends) - trajectory_ends
    end_total = jnp.sum(trajectory_ends)
    opened = before == 0
    closed = end_total - before == 0
    positions = jnp.arange(row_count, dtype=jnp.int32)
    pair_mask = (positions[None, :] <= positions[:, None]) & (before[:, None] == before[None, :])
    reset_any = (end_total > 0).astype(jnp.float32).reshape(1)
    open_bf = opened.astype(jnp.bfloat16)[:, None, None]
    close_bf = closed.astype(jnp.bfloat16)[:, None, None]
    carry_out = jnp.einsum(
        "shv,shk->hvk", value_rows * close_bf, key_rows, preferred_element_type=jnp.float32
    )
    grads_out = jnp.einsum(
        "thv,thk->hvk", grad_rows * open_bf, queries, preferred_element_type=jnp.float32
    )
    zero_state = jnp.zeros((head_count, HD, HD), jnp.float32)
    zero_flag = jnp.zeros((1,), jnp.float32)
    flag_list = lax.all_gather(reset_any, "ctx", axis=0, tiled=True)
    own_index = lax.axis_index("ctx")
    order = jnp.arange(flag_list.shape[0], dtype=jnp.int32)
    start_from = jnp.max(jnp.where((order < own_index) & (flag_list > 0), order, 0))
    piece = lax.all_gather(carry_out[None], "ctx", axis=0, tiled=True)
    index_list = jnp.arange(piece.shape[0], dtype=jnp.int32)
    weights = ((index_list >= start_from) & (index_list < own_index)).astype(jnp.float32)
    state_in = jnp.sum(weights[:, None, None, None] * piece, axis=0)
    grads_in = prefix((grads_out, reset_any), "ctx", joined, (zero_state, zero_flag))[0]
    scores = jnp.einsum("thv,shv->hts", grad_rows, value_rows, preferred_element_type=jnp.float32)
    scores = jnp.where(pair_mask[None], scores, 0.0).astype(jnp.bfloat16)
    attn = jnp.einsum("thk,shk->hts", queries, key_rows, preferred_element_type=jnp.float32)
    attn = jnp.where(pair_mask[None], attn, 0.0).astype(jnp.bfloat16)
    state_bf = state_in.astype(jnp.bfloat16)
    grads_bf = grads_in.astype(jnp.bfloat16)
    open_f = opened.astype(jnp.float32)[:, None, None]
    close_f = closed.astype(jnp.float32)[:, None, None]
    score_scale = 1.0 / HD
    grad_query = jnp.einsum("hts,shk->thk", scores, key_rows, preferred_element_type=jnp.float32)
    grad_query = grad_query + open_f * jnp.einsum(
        "thv,hvk->thk", grad_rows, state_bf, preferred_element_type=jnp.float32
    )
    grad_key = jnp.einsum("hts,thk->shk", scores, queries, preferred_element_type=jnp.float32)
    grad_key = grad_key + close_f * jnp.einsum(
        "shv,hvk->shk", value_rows, grads_bf, preferred_element_type=jnp.float32
    )
    grad_value = jnp.einsum("hts,thv->shv", attn, grad_rows, preferred_element_type=jnp.float32)
    grad_value = grad_value + close_f * jnp.einsum(
        "shk,hvk->shv", key_rows, grads_bf, preferred_element_type=jnp.float32
    )
    flat = (row_count, head_count * HD)
    grad_query = (score_scale * grad_query).astype(jnp.bfloat16).reshape(flat)
    grad_key = (score_scale * grad_key).astype(jnp.bfloat16).reshape(flat)
    grad_value = (score_scale * grad_value).astype(jnp.bfloat16).reshape(flat)
    dims = (((1,), (1,)), ((), ()))
    total = lax.dot_general(grad_query, w_query, dims, preferred_element_type=jnp.float32)
    total = total + lax.dot_general(grad_key, w_key, dims, preferred_element_type=jnp.float32)
    total = total + lax.dot_general(grad_value, w_value, dims, preferred_element_type=jnp.float32)
    shares = lax.psum_scatter(total, "tp", scatter_dimension=0, tiled=True)
    return shares.astype(jnp.bfloat16)


NN = ((1,), (0,))
NT = ((1,), (1,))
TN = ((0,), (0,))
COLS = 256
SPLIT = 2
BF = jnp.bfloat16
F32 = jnp.float32


def dot(a, b, dims):
    return lax.dot_general(a, b, (dims, ((), ())), preferred_element_type=F32)


def fused(
    nc, nt, tok_hbm, wq_hbm, wk_hbm, wv_hbm, g_hbm, ends_ref, out_ref,
    tok, w, g, qkv, mask, openc, closec, acc, dcat,
    st, fl, xfl, xr, cr, co, bs, br, fin,
    kept, sent, recd, ysent, yrecd,
    load_sem, fl_sem, x_send, x_recv, c_send, c_recv, b_send, b_recv,
    rs_send, rs_recv, y_send, y_recv,
):
    rows, width = tok.shape
    heads = g.shape[0]
    half = heads // 2
    pieces = half * SPLIT
    deep = HD // SPLIT
    chunks = width // COLS
    share = rows // nt
    ctx = lax.axis_index("ctx")
    tp = lax.axis_index("tp")
    par, pair = ctx % 2, ctx // 2
    pairs = nc // 2
    lo, hi = tp % 2, tp // 2
    mate = ctx + 1 - 2 * par
    core = tp + 1 - 2 * lo
    over = tp + 2 - 4 * hi

    turn = jnp.where(pair >= pairs // 2, 1, 0)
    token_load = pltpu.make_async_copy(tok_hbm, tok, load_sem.at[0])
    weight_loads = [
        pltpu.make_async_copy(ref, w.at[n], load_sem.at[1 + n])
        for n, ref in enumerate((wq_hbm, wk_hbm, wv_hbm))
    ]
    g_loads = [
        pltpu.make_async_copy(g_hbm.at[:, pl.ds(h * HD, HD)], g.at[h], load_sem.at[4 + h])
        for h in range(heads)
    ]
    token_load.start()

    @pl.when(turn == 0)
    def _():
        for n in (1, 2, 0):
            weight_loads[n].start()
        for load in g_loads:
            load.start()

    @pl.when(turn == 1)
    def _():
        weight_loads[0].start()
        for load in g_loads:
            load.start()
        for n in (1, 2):
            weight_loads[n].start()

    barrier = pltpu.get_barrier_semaphore()
    pl.semaphore_signal(barrier, inc=1, device_id={"ctx": mate}, device_id_type=pl.DeviceIdType.MESH)
    pl.semaphore_signal(barrier, inc=1, device_id={"tp": core}, device_id_type=pl.DeviceIdType.MESH)
    pl.semaphore_signal(barrier, inc=1, device_id={"tp": over}, device_id_type=pl.DeviceIdType.MESH)

    @pl.when(pair > 0)
    def _():
        pl.semaphore_signal(
            barrier, inc=1, device_id={"ctx": ctx - 2}, device_id_type=pl.DeviceIdType.MESH
        )

    @pl.when(pair < pairs - 1)
    def _():
        pl.semaphore_signal(
            barrier, inc=1, device_id={"ctx": ctx + 2}, device_id_type=pl.DeviceIdType.MESH
        )

    def remote(src, dst, send, recv, device):
        return pltpu.make_async_remote_copy(
            src_ref=src, dst_ref=dst, send_sem=send, recv_sem=recv,
            device_id=device, device_id_type=pl.DeviceIdType.MESH,
        )

    ends_row = jnp.broadcast_to(ends_ref[...].astype(F32), (HD, rows)).astype(BF)
    row_id = lax.broadcasted_iota(jnp.int32, (rows, rows), 0)
    col_id = lax.broadcasted_iota(jnp.int32, (rows, rows), 1)
    below = (row_id < col_id).astype(F32).astype(BF)
    above = (col_id < row_id).astype(F32).astype(BF)
    before_row = dot(ends_row, below, NN)[0:1, :]
    before_col = dot(above, ends_row, NT)
    total = jnp.sum(ends_ref[...].astype(F32), axis=1, keepdims=True)
    openc[...] = (before_col == 0.0).astype(F32)
    closec[...] = (jnp.broadcast_to(total, (rows, HD)) == before_col).astype(F32)
    fl[...] = jnp.broadcast_to((total > 0.0).astype(F32), fl.shape)
    same = before_row == jnp.broadcast_to(before_col[:, 0:1], (rows, rows))
    mask[...] = jnp.where(same & (col_id <= row_id), 1.0, 0.0)

    waits = 3 + jnp.where(pair > 0, 1, 0) + jnp.where(pair < pairs - 1, 1, 0)
    pl.semaphore_wait(barrier, waits)
    flag_copy = remote(fl, xfl, fl_sem.at[0], fl_sem.at[1], {"ctx": mate})
    flag_copy.start()

    block = min(256, rows)
    spans = [(at, at + block) for at in range(0, rows, block)]

    def project(which):
        @pl.loop(0, rows // block)
        def _(step):
            at = pl.ds(pl.multiple_of(step * block, block), block)
            made = dot(tok[at, :], w[which], NN).astype(BF)
            for h in range(heads):
                qkv[which, h, at, :] = made[:, h * HD : (h + 1) * HD]

    def x_copy(d, i):
        return remote(
            st.at[d, (1 - par) * pieces + i], xr.at[d, i],
            x_send.at[d, i], x_recv.at[d, i], {"ctx": mate},
        )

    def state(d, h):
        if d == 0:
            made = dot(qkv[2, h] * closec[...].astype(BF), qkv[1, h], TN)
        else:
            made = dot(g[h] * openc[...].astype(BF), qkv[0, h], TN)
        for n in range(SPLIT):
            st[d, h * SPLIT + n] = made[n * deep : (n + 1) * deep]

    def give(d):
        for i in range(half):
            state(d, (1 - par) * half + i)
            for n in range(SPLIT):
                x_copy(d, i * SPLIT + n).start()

    def forward_part():
        for n in (1, 2):
            weight_loads[n].wait()
            project(n)
        give(0)

    def backward_part():
        weight_loads[0].wait()
        project(0)
        for load in g_loads:
            load.wait()
        give(1)

    token_load.wait()

    @pl.when(turn == 0)
    def _():
        forward_part()
        backward_part()

    @pl.when(turn == 1)
    def _():
        backward_part()
        forward_part()

    for i in range(half):
        state(0, par * half + i)
        state(1, par * half + i)

    def within(h):
        for n, (start, stop) in enumerate(spans):
            at, upto = slice(start, stop), slice(0, stop)
            keep = mask[at, upto]
            scores = (dot(g[h, at, :], qkv[2, h, upto, :], NT) * keep).astype(BF)
            attn = (dot(qkv[0, h, at, :], qkv[1, h, upto, :], NT) * keep).astype(BF)
            acc[0, h, at, :] = dot(scores, qkv[1, h, upto, :], NN)
            dk = dot(scores, qkv[0, h, at, :], TN)
            dv = dot(attn, g[h, at, :], TN)
            if n:
                old = slice(0, start)
                acc[1, h, old, :] += dk[old]
                acc[2, h, old, :] += dv[old]
            acc[1, h, at, :] = dk[at]
            acc[2, h, at, :] = dv[at]

    def within_some(first, last):
        @pl.loop(first, last)
        def _(h):
            within(h)

    def c_copy(d, i):
        return remote(
            co.at[d, i], cr.at[d, i], c_send.at[d, i], c_recv.at[d, i],
            {"ctx": ctx + 2 - 4 * d},
        )

    def b_copy(d, i):
        return remote(bs.at[d, i], br.at[d, i], b_send.at[d, i], b_recv.at[d, i], {"ctx": mate})

    def has_next(d):
        return ((d == 0) & (pair < pairs - 1)) | ((d == 1) & (pair > 0))

    def has_prev(d):
        return ((d == 0) & (pair > 0)) | ((d == 1) & (pair < pairs - 1))

    def place(i):
        return slice(i % SPLIT * deep, (i % SPLIT + 1) * deep)

    def carry(d):
        first_here = par == d
        more, begun = has_next(d), has_prev(d)
        own_flag, mate_flag = fl[0:1, :], xfl[0:1, :]
        first_flag = jnp.where(first_here, own_flag, mate_flag)
        second_flag = jnp.where(first_here, mate_flag, own_flag)

        @pl.when(jnp.logical_not(begun))
        def _():
            cr[d] = jnp.zeros(cr.shape[1:], F32)

        for i in range(pieces):
            x_copy(d, i).wait_recv()
            own, other = st[d, par * pieces + i], xr[d, i]
            first = jnp.where(first_here, own, other)
            second = jnp.where(first_here, other, own)

            @pl.when(begun)
            def _():
                c_copy(d, i).wait_recv()

            into = cr[d, i]
            inner = first + (1.0 - first_flag) * into

            @pl.when(more)
            def _():
                co[d, i] = second + (1.0 - second_flag) * inner
                c_copy(d, i).start()

            bs[d, i] = jnp.where(first_here, inner, into)
            b_copy(d, i).start()
            mine = jnp.where(first_here, into, inner).astype(BF)
            fin[d, par * half + i // SPLIT, place(i), :] = mine

    cut = half + half // 2
    within_some(0, half)
    flag_copy.wait_recv()
    carry(turn)
    within_some(half, cut)
    carry(1 - turn)
    within_some(cut, heads)

    scale = 1.0 / HD

    def finish(d, h):
        at = pl.ds(pl.multiple_of(h * HD, HD), HD)

        @pl.when(d == 0)
        def _():
            dq = acc[0, h] + openc[...] * dot(g[h], fin[0, h], NN)
            dcat[0, :, at] = (scale * dq).astype(BF)

        @pl.when(d == 1)
        def _():
            b_in, closed = fin[1, h], closec[...]
            dk = acc[1, h] + closed * dot(qkv[2, h], b_in, NN)
            dv = acc[2, h] + closed * dot(qkv[1, h], b_in, NT)
            dcat[1, :, at] = (scale * dk).astype(BF)
            dcat[2, :, at] = (scale * dv).astype(BF)

    @pl.loop(0, 2 * half)
    def _(n):
        finish((n // half + turn) % 2, par * half + n % half)

    for d in (turn, 1 - turn):
        for i in range(half):
            h = (1 - par) * half + i
            for n in range(i * SPLIT, (i + 1) * SPLIT):
                b_copy(d, n).wait_recv()
                fin[d, h, place(n), :] = br[d, n].astype(BF)
            finish(d, h)

    def rs_copy(part, j):
        return remote(
            sent.at[part, j], recd.at[part, j], rs_send.at[part, j], rs_recv.at[part, j],
            {"tp": core},
        )

    def y_copy(j):
        return remote(ysent.at[j], yrecd.at[j], y_send.at[j], y_recv.at[j], {"tp": over})

    def product(part, j):
        side = jnp.where(part == 0, 1 - hi, hi)
        at = pl.ds(pl.multiple_of(side * 2 * share, 2 * share), 2 * share)
        cols = pl.ds(pl.multiple_of(j * COLS, COLS), COLS)
        made = dot(dcat[0, at, :], w[0, cols, :], NT)
        made = made + dot(dcat[1, at, :], w[1, cols, :], NT)
        made = made + dot(dcat[2, at, :], w[2, cols, :], NT)
        low, high = made[0:share], made[share : 2 * share]
        sent[part, j] = jnp.where(lo == 0, high, low)
        kept[part, j] = jnp.where(lo == 0, low, high)
        rs_copy(part, j).start()

    def pass_on(j):
        rs_copy(0, j).wait_recv()
        ysent[j] = kept[0, j] + recd[0, j]
        y_copy(j).start()

    product(0, 0)

    @pl.loop(1, chunks)
    def _(j):
        product(0, j)
        pass_on(j - 1)

    product(1, 0)
    pass_on(chunks - 1)

    @pl.loop(1, chunks)
    def _(j):
        product(1, j)

    for j in range(chunks):
        rs_copy(1, j).wait_recv()
        y_copy(j).wait_recv()
        out_ref[:, j * COLS : (j + 1) * COLS] = (kept[1, j] + recd[1, j] + yrecd[j]).astype(BF)

    flag_copy.wait_send()
    for d in range(2):
        for i in range(pieces):
            x_copy(d, i).wait_send()
            b_copy(d, i).wait_send()

        @pl.when(has_next(d))
        def _():
            for i in range(pieces):
                c_copy(d, i).wait_send()

    @pl.loop(0, chunks)
    def _(j):
        rs_copy(0, j).wait_send()
        rs_copy(1, j).wait_send()
        y_copy(j).wait_send()


def fused_body(nc, nt, tokens_in, w_query, w_key, w_value, grad_out, trajectory_ends):
    rows, width = tokens_in.shape
    inner = w_query.shape[1]
    heads = inner // HD
    half = heads // 2
    share = rows // nt
    chunks = width // COLS
    anywhere = pl.BlockSpec(memory_space=pl.ANY)
    vmem = pl.BlockSpec(memory_space=pltpu.VMEM)
    dma = pltpu.SemaphoreType.DMA
    pieces = half * SPLIT
    deep = HD // SPLIT
    states = pltpu.VMEM((2, pieces, deep, HD), F32)
    piece = (chunks, share, COLS)
    return pl.pallas_call(
        functools.partial(fused, nc, nt),
        out_shape=jax.ShapeDtypeStruct((share, width), BF),
        in_specs=[anywhere] * 5 + [vmem],
        out_specs=vmem,
        scratch_shapes=[
            pltpu.VMEM((rows, width), BF),
            pltpu.VMEM((3, width, inner), BF),
            pltpu.VMEM((heads, rows, HD), BF),
            pltpu.VMEM((3, heads, rows, HD), BF),
            pltpu.VMEM((rows, rows), F32),
            pltpu.VMEM((rows, HD), F32),
            pltpu.VMEM((rows, HD), F32),
            pltpu.VMEM((3, heads, rows, HD), F32),
            pltpu.VMEM((3, rows, inner), BF),
            pltpu.VMEM((2, heads * SPLIT, deep, HD), F32),
            pltpu.VMEM((8, HD), F32),
            pltpu.VMEM((8, HD), F32),
            states, states, states, states, states,
            pltpu.VMEM((2, heads, HD, HD), BF),
            pltpu.VMEM((2, *piece), F32),
            pltpu.VMEM((2, *piece), F32),
            pltpu.VMEM((2, *piece), F32),
            pltpu.VMEM(piece, F32),
            pltpu.VMEM(piece, F32),
            dma((4 + heads,)),
            dma((2,)),
            dma((2, pieces)), dma((2, pieces)),
            dma((2, pieces)), dma((2, pieces)),
            dma((2, pieces)), dma((2, pieces)),
            dma((2, chunks)), dma((2, chunks)),
            dma((chunks,)), dma((chunks,)),
        ],
        compiler_params=pltpu.CompilerParams(
            collective_id=0, has_side_effects=True, vmem_limit_bytes=60 * 2**20
        ),
    )(tokens_in, w_query, w_key, w_value, grad_out, trajectory_ends.reshape(1, rows))


def solution(mesh):
    nc, nt = mesh.shape["ctx"], mesh.shape["tp"]

    def local(tokens_in, w_query, w_key, w_value, grad_out, trajectory_ends):
        rows, width = tokens_in.shape
        heads = w_query.shape[1] // HD
        fits = nt == 4 and nc % 2 == 0 and heads % 2 == 0 and rows <= 512
        fits = fits and width % COLS == 0 and rows % 256 == 0
        call = functools.partial(fused_body, nc, nt) if fits else body
        return call(tokens_in, w_query, w_key, w_value, grad_out, trajectory_ends)

    return jax.shard_map(
        local,
        mesh=mesh,
        in_specs=(
            P("ctx", None),
            P(None, "tp"),
            P(None, "tp"),
            P(None, "tp"),
            P("ctx", "tp"),
            P("ctx"),
        ),
        out_specs=P(("ctx", "tp"), None),
        check_vma=False,
    )
```

```python
import functools

import jax
import jax.numpy as jnp
from jax import lax
from jax.experimental import pallas as pl
from jax.experimental.pallas import tpu as pltpu
from jax.sharding import PartitionSpec as P

HD = 128


def prefix(part, axis, combine, identity):
    count = lax.axis_size(axis)
    place = lax.axis_index(axis)
    ahead = count - 1 - place
    gathered = jax.tree.map(lambda a: lax.all_gather(a, axis), part)
    state = jax.tree.map(lambda a, e: jnp.zeros_like(a) + jnp.asarray(e, a.dtype), part, identity)

    def one(hop, state):
        source = count - 1 - hop
        return combine(
            state, jax.tree.map(lambda a: lax.dynamic_index_in_dim(a, source, 0, False), gathered)
        )

    return lax.fori_loop(0, ahead, one, state)


def joined(earlier, later):
    return (later[0] + (1.0 - later[1][0]) * earlier[0], jnp.maximum(earlier[1], later[1]))


def body(tokens_in, w_query, w_key, w_value, grad_out, trajectory_ends):
    row_count = tokens_in.shape[0]
    head_count = w_query.shape[1] // HD
    shape = (row_count, head_count, HD)
    queries = (
        jnp.dot(tokens_in, w_query, preferred_element_type=jnp.float32)
        .astype(jnp.bfloat16)
        .reshape(shape)
    )
    key_rows = (
        jnp.dot(tokens_in, w_key, preferred_element_type=jnp.float32)
        .astype(jnp.bfloat16)
        .reshape(shape)
    )
    value_rows = (
        jnp.dot(tokens_in, w_value, preferred_element_type=jnp.float32)
        .astype(jnp.bfloat16)
        .reshape(shape)
    )
    grad_rows = grad_out.reshape(shape)
    before = jnp.cumsum(trajectory_ends) - trajectory_ends
    end_total = jnp.sum(trajectory_ends)
    opened = before == 0
    closed = end_total - before == 0
    positions = jnp.arange(row_count, dtype=jnp.int32)
    pair_mask = (positions[None, :] <= positions[:, None]) & (before[:, None] == before[None, :])
    reset_any = (end_total > 0).astype(jnp.float32).reshape(1)
    open_bf = opened.astype(jnp.bfloat16)[:, None, None]
    close_bf = closed.astype(jnp.bfloat16)[:, None, None]
    carry_out = jnp.einsum(
        "shv,shk->hvk", value_rows * close_bf, key_rows, preferred_element_type=jnp.float32
    )
    grads_out = jnp.einsum(
        "thv,thk->hvk", grad_rows * open_bf, queries, preferred_element_type=jnp.float32
    )
    zero_state = jnp.zeros((head_count, HD, HD), jnp.float32)
    zero_flag = jnp.zeros((1,), jnp.float32)
    flag_list = lax.all_gather(reset_any, "ctx", axis=0, tiled=True)
    own_index = lax.axis_index("ctx")
    order = jnp.arange(flag_list.shape[0], dtype=jnp.int32)
    start_from = jnp.max(jnp.where((order < own_index) & (flag_list > 0), order, 0))
    piece = lax.all_gather(carry_out[None], "ctx", axis=0, tiled=True)
    index_list = jnp.arange(piece.shape[0], dtype=jnp.int32)
    weights = ((index_list >= start_from) & (index_list < own_index)).astype(jnp.float32)
    state_in = jnp.sum(weights[:, None, None, None] * piece, axis=0)
    grads_in = prefix((grads_out, reset_any), "ctx", joined, (zero_state, zero_flag))[0]
    scores = jnp.einsum("thv,shv->hts", grad_rows, value_rows, preferred_element_type=jnp.float32)
    scores = jnp.where(pair_mask[None], scores, 0.0).astype(jnp.bfloat16)
    attn = jnp.einsum("thk,shk->hts", queries, key_rows, preferred_element_type=jnp.float32)
    attn = jnp.where(pair_mask[None], attn, 0.0).astype(jnp.bfloat16)
    state_bf = state_in.astype(jnp.bfloat16)
    grads_bf = grads_in.astype(jnp.bfloat16)
    open_f = opened.astype(jnp.float32)[:, None, None]
    close_f = closed.astype(jnp.float32)[:, None, None]
    score_scale = 1.0 / HD
    grad_query = jnp.einsum("hts,shk->thk", scores, key_rows, preferred_element_type=jnp.float32)
    grad_query = grad_query + open_f * jnp.einsum(
        "thv,hvk->thk", grad_rows, state_bf, preferred_element_type=jnp.float32
    )
    grad_key = jnp.einsum("hts,thk->shk", scores, queries, preferred_element_type=jnp.float32)
    grad_key = grad_key + close_f * jnp.einsum(
        "shv,hvk->shk", value_rows, grads_bf, preferred_element_type=jnp.float32
    )
    grad_value = jnp.einsum("hts,thv->shv", attn, grad_rows, preferred_element_type=jnp.float32)
    grad_value = grad_value + close_f * jnp.einsum(
        "shk,hvk->shv", key_rows, grads_bf, preferred_element_type=jnp.float32
    )
    flat = (row_count, head_count * HD)
    grad_query = (score_scale * grad_query).astype(jnp.bfloat16).reshape(flat)
    grad_key = (score_scale * grad_key).astype(jnp.bfloat16).reshape(flat)
    grad_value = (score_scale * grad_value).astype(jnp.bfloat16).reshape(flat)
    dims = (((1,), (1,)), ((), ()))
    total = lax.dot_general(grad_query, w_query, dims, preferred_element_type=jnp.float32)
    total = total + lax.dot_general(grad_key, w_key, dims, preferred_element_type=jnp.float32)
    total = total + lax.dot_general(grad_value, w_value, dims, preferred_element_type=jnp.float32)
    shares = lax.psum_scatter(total, "tp", scatter_dimension=0, tiled=True)
    return shares.astype(jnp.bfloat16)


NN = ((1,), (0,))
NT = ((1,), (1,))
TN = ((0,), (0,))
COLS = 256
SPLIT = 2
BF = jnp.bfloat16
F32 = jnp.float32


def dot(a, b, dims):
    return lax.dot_general(a, b, (dims, ((), ())), preferred_element_type=F32)


def fused(
    nc, nt, tok_hbm, wq_hbm, wk_hbm, wv_hbm, g_hbm, ends_hbm, out_ref,
    ends_ref, tok, w, g, qkv, mask, flip, openc, closec, acc, dcat,
    st, fl, xfl, xr, cr, co, bs, br, fin,
    kept, sent, recd, ysent, yrecd,
    load_sem, fl_sem, x_send, x_recv, c_send, c_recv, b_send, b_recv,
    rs_send, rs_recv, y_send, y_recv,
):
    rows, width = tok.shape
    heads = g.shape[0]
    half = heads // 2
    pieces = half * SPLIT
    deep = HD // SPLIT
    chunks = width // COLS
    share = rows // nt
    ctx = lax.axis_index("ctx")
    tp = lax.axis_index("tp")
    par, pair = ctx % 2, ctx // 2
    pairs = nc // 2
    lo, hi = tp % 2, tp // 2
    mate = ctx + 1 - 2 * par
    core = tp + 1 - 2 * lo
    over = tp + 2 - 4 * hi

    turn = jnp.where(pair >= pairs // 2, 1, 0)
    token_load = pltpu.make_async_copy(tok_hbm, tok, load_sem.at[0])
    weight_loads = [
        pltpu.make_async_copy(ref, w.at[n], load_sem.at[1 + n])
        for n, ref in enumerate((wq_hbm, wk_hbm, wv_hbm))
    ]
    g_loads = [
        pltpu.make_async_copy(g_hbm.at[:, pl.ds(h * HD, HD)], g.at[h], load_sem.at[4 + h])
        for h in range(heads)
    ]
    ends_load = pltpu.make_async_copy(ends_hbm, ends_ref, load_sem.at[4 + heads])
    ends_load.start()
    token_load.start()

    @pl.when(turn == 0)
    def _():
        for n in (1, 2, 0):
            weight_loads[n].start()
        for load in g_loads:
            load.start()

    @pl.when(turn == 1)
    def _():
        weight_loads[0].start()
        for load in g_loads:
            load.start()
        for n in (1, 2):
            weight_loads[n].start()

    barrier = pltpu.get_barrier_semaphore()
    pl.semaphore_signal(barrier, inc=1, device_id={"ctx": mate}, device_id_type=pl.DeviceIdType.MESH)
    pl.semaphore_signal(barrier, inc=1, device_id={"tp": core}, device_id_type=pl.DeviceIdType.MESH)
    pl.semaphore_signal(barrier, inc=1, device_id={"tp": over}, device_id_type=pl.DeviceIdType.MESH)

    @pl.when(pair > 0)
    def _():
        pl.semaphore_signal(
            barrier, inc=1, device_id={"ctx": ctx - 2}, device_id_type=pl.DeviceIdType.MESH
        )

    @pl.when(pair < pairs - 1)
    def _():
        pl.semaphore_signal(
            barrier, inc=1, device_id={"ctx": ctx + 2}, device_id_type=pl.DeviceIdType.MESH
        )

    def remote(src, dst, send, recv, device):
        return pltpu.make_async_remote_copy(
            src_ref=src, dst_ref=dst, send_sem=send, recv_sem=recv,
            device_id=device, device_id_type=pl.DeviceIdType.MESH,
        )

    ends_load.wait()
    ends_row = jnp.broadcast_to(ends_ref[...].astype(F32), (HD, rows)).astype(BF)
    row_id = lax.broadcasted_iota(jnp.int32, (rows, rows), 0)
    col_id = lax.broadcasted_iota(jnp.int32, (rows, rows), 1)
    below = (row_id < col_id).astype(F32).astype(BF)
    above = (col_id < row_id).astype(F32).astype(BF)
    before_row = dot(ends_row, below, NN)[0:1, :]
    before_col = dot(above, ends_row, NT)
    total = jnp.sum(ends_ref[...].astype(F32), axis=1, keepdims=True)
    openc[...] = (before_col == 0.0).astype(F32)
    closec[...] = (jnp.broadcast_to(total, (rows, HD)) == before_col).astype(F32)
    fl[...] = jnp.broadcast_to((total > 0.0).astype(F32), fl.shape)
    same = before_row == jnp.broadcast_to(before_col[:, 0:1], (rows, rows))
    mask[...] = (same & (col_id <= row_id)).astype(F32).astype(BF)
    flip[...] = (same & (row_id <= col_id)).astype(F32).astype(BF)

    block = min(256, rows)
    spans = [(at, at + block) for at in range(0, rows, block)]

    def project(which):
        @pl.loop(0, rows // block)
        def _(step):
            at = pl.ds(pl.multiple_of(step * block, block), block)
            made = dot(tok[at, :], w[which], NN).astype(BF)
            for h in range(heads):
                qkv[which, h, at, :] = made[:, h * HD : (h + 1) * HD]

    def x_copy(d, i):
        return remote(
            st.at[d, (1 - par) * pieces + i], xr.at[d, i],
            x_send.at[d, i], x_recv.at[d, i], {"ctx": mate},
        )

    def state(d, h):
        if d == 0:
            made = dot(qkv[2, h] * closec[...].astype(BF), qkv[1, h], TN)
        else:
            made = dot(g[h] * openc[...].astype(BF), qkv[0, h], TN)
        for n in range(SPLIT):
            st[d, h * SPLIT + n] = made[n * deep : (n + 1) * deep]

    def give(d):
        for i in range(half):
            state(d, (1 - par) * half + i)
            for n in range(SPLIT):
                x_copy(d, i * SPLIT + n).start()

    def keys_values():
        for n in (1, 2):
            weight_loads[n].wait()
            project(n)

    def queries():
        weight_loads[0].wait()
        project(0)

    token_load.wait()

    @pl.when(turn == 0)
    def _():
        keys_values()

    @pl.when(turn == 1)
    def _():
        queries()

    for load in g_loads:
        load.wait()
    waits = 3 + jnp.where(pair > 0, 1, 0) + jnp.where(pair < pairs - 1, 1, 0)
    pl.semaphore_wait(barrier, waits)
    flag_copy = remote(fl, xfl, fl_sem.at[0], fl_sem.at[1], {"ctx": mate})
    flag_copy.start()

    @pl.when(turn == 0)
    def _():
        give(0)
        queries()
        give(1)

    @pl.when(turn == 1)
    def _():
        give(1)
        keys_values()
        give(0)

    for i in range(half):
        state(0, par * half + i)
        state(1, par * half + i)

    def within(h):
        for start, stop in spans:
            at, upto, onward = slice(start, stop), slice(0, stop), slice(start, rows)
            scores = dot(g[h, at, :], qkv[2, h, upto, :], NT).astype(BF) * mask[at, upto]
            acc[0, h, at, :] = dot(scores, qkv[1, h, upto, :], NN)
            turned = dot(qkv[2, h, at, :], g[h, onward, :], NT).astype(BF) * flip[at, onward]
            acc[1, h, at, :] = dot(turned, qkv[0, h, onward, :], NN)
            attn = dot(qkv[1, h, at, :], qkv[0, h, onward, :], NT).astype(BF) * flip[at, onward]
            acc[2, h, at, :] = dot(attn, g[h, onward, :], NN)

    def within_some(first, last):
        @pl.loop(first, last)
        def _(h):
            within(h)

    def c_copy(d, i):
        return remote(
            co.at[d, i], cr.at[d, i], c_send.at[d, i], c_recv.at[d, i],
            {"ctx": ctx + 2 - 4 * d},
        )

    def b_copy(d, i):
        return remote(bs.at[d, i], br.at[d, i], b_send.at[d, i], b_recv.at[d, i], {"ctx": mate})

    def has_next(d):
        return ((d == 0) & (pair < pairs - 1)) | ((d == 1) & (pair > 0))

    def has_prev(d):
        return ((d == 0) & (pair > 0)) | ((d == 1) & (pair < pairs - 1))

    def place(i):
        return slice(i % SPLIT * deep, (i % SPLIT + 1) * deep)

    def carry(d):
        first_here = par == d
        more, begun = has_next(d), has_prev(d)
        own_flag, mate_flag = fl[0:1, :], xfl[0:1, :]
        first_flag = jnp.where(first_here, own_flag, mate_flag)
        second_flag = jnp.where(first_here, mate_flag, own_flag)

        @pl.when(jnp.logical_not(begun))
        def _():
            cr[d] = jnp.zeros(cr.shape[1:], F32)

        for i in range(pieces):
            x_copy(d, i).wait_recv()
            own, other = st[d, par * pieces + i], xr[d, i]
            first = jnp.where(first_here, own, other)
            second = jnp.where(first_here, other, own)

            @pl.when(begun)
            def _():
                c_copy(d, i).wait_recv()

            into = cr[d, i]
            inner = first + (1.0 - first_flag) * into

            @pl.when(more)
            def _():
                co[d, i] = second + (1.0 - second_flag) * inner
                c_copy(d, i).start()

            bs[d, i] = jnp.where(first_here, inner, into)
            b_copy(d, i).start()
            mine = jnp.where(first_here, into, inner).astype(BF)
            fin[d, par * half + i // SPLIT, place(i), :] = mine

    at_end = (pair == 0) | (pair == pairs - 1)
    early = jnp.where(at_end, 0, heads // 4)
    late = jnp.where(at_end, heads - heads // 4, heads // 2)
    flag_copy.wait_recv()
    within_some(0, early)
    carry(turn)
    within_some(early, late)
    carry(1 - turn)
    within_some(late, heads)

    scale = 1.0 / HD

    def finish(d, h):
        at = pl.ds(pl.multiple_of(h * HD, HD), HD)

        @pl.when(d == 0)
        def _():
            dq = acc[0, h] + openc[...] * dot(g[h], fin[0, h], NN)
            dcat[0, :, at] = (scale * dq).astype(BF)

        @pl.when(d == 1)
        def _():
            b_in, closed = fin[1, h], closec[...]
            dk = acc[1, h] + closed * dot(qkv[2, h], b_in, NN)
            dv = acc[2, h] + closed * dot(qkv[1, h], b_in, NT)
            dcat[1, :, at] = (scale * dk).astype(BF)
            dcat[2, :, at] = (scale * dv).astype(BF)

    @pl.loop(0, 2 * half)
    def _(n):
        finish((n // half + turn) % 2, par * half + n % half)

    for d in (turn, 1 - turn):
        for i in range(half):
            h = (1 - par) * half + i
            for n in range(i * SPLIT, (i + 1) * SPLIT):
                b_copy(d, n).wait_recv()
                fin[d, h, place(n), :] = br[d, n].astype(BF)
            finish(d, h)

    def rs_copy(part, j):
        return remote(
            sent.at[part, j], recd.at[part, j], rs_send.at[part, j], rs_recv.at[part, j],
            {"tp": core},
        )

    def y_copy(j):
        return remote(ysent.at[j], yrecd.at[j], y_send.at[j], y_recv.at[j], {"tp": over})

    def product(part, j):
        side = jnp.where(part == 0, 1 - hi, hi)
        at = pl.ds(pl.multiple_of(side * 2 * share, 2 * share), 2 * share)
        cols = pl.ds(pl.multiple_of(j * COLS, COLS), COLS)
        made = dot(dcat[0, at, :], w[0, cols, :], NT)
        made = made + dot(dcat[1, at, :], w[1, cols, :], NT)
        made = made + dot(dcat[2, at, :], w[2, cols, :], NT)
        low, high = made[0:share], made[share : 2 * share]
        sent[part, j] = jnp.where(lo == 0, high, low)
        kept[part, j] = jnp.where(lo == 0, low, high)
        rs_copy(part, j).start()

    def pass_on(j):
        rs_copy(0, j).wait_recv()
        ysent[j] = kept[0, j] + recd[0, j]
        y_copy(j).start()

    product(0, 0)

    @pl.loop(1, chunks)
    def _(j):
        product(0, j)
        pass_on(j - 1)

    product(1, 0)
    pass_on(chunks - 1)

    @pl.loop(1, chunks)
    def _(j):
        product(1, j)

    for j in range(chunks):
        rs_copy(1, j).wait_recv()
        y_copy(j).wait_recv()
        out_ref[:, j * COLS : (j + 1) * COLS] = (kept[1, j] + recd[1, j] + yrecd[j]).astype(BF)

    flag_copy.wait_send()
    for d in range(2):
        for i in range(pieces):
            x_copy(d, i).wait_send()
            b_copy(d, i).wait_send()

        @pl.when(has_next(d))
        def _():
            for i in range(pieces):
                c_copy(d, i).wait_send()

    @pl.loop(0, chunks)
    def _(j):
        rs_copy(0, j).wait_send()
        rs_copy(1, j).wait_send()
        y_copy(j).wait_send()


def fused_body(nc, nt, tokens_in, w_query, w_key, w_value, grad_out, trajectory_ends):
    rows, width = tokens_in.shape
    inner = w_query.shape[1]
    heads = inner // HD
    half = heads // 2
    share = rows // nt
    chunks = width // COLS
    outside = pl.BlockSpec(memory_space=pltpu.HBM)
    vmem = pl.BlockSpec(memory_space=pltpu.VMEM)
    dma = pltpu.SemaphoreType.DMA
    pieces = half * SPLIT
    deep = HD // SPLIT
    states = pltpu.VMEM((2, pieces, deep, HD), F32)
    piece = (chunks, share, COLS)
    operands = (tokens_in, w_query, w_key, w_value, grad_out, trajectory_ends.reshape(1, rows))
    return pl.pallas_call(
        functools.partial(fused, nc, nt),
        out_shape=jax.ShapeDtypeStruct((share, width), BF),
        in_specs=[outside] * 6,
        out_specs=vmem,
        scratch_shapes=[
            pltpu.VMEM((1, rows), jnp.int32),
            pltpu.VMEM((rows, width), BF),
            pltpu.VMEM((3, width, inner), BF),
            pltpu.VMEM((heads, rows, HD), BF),
            pltpu.VMEM((3, heads, rows, HD), BF),
            pltpu.VMEM((rows, rows), BF),
            pltpu.VMEM((rows, rows), BF),
            pltpu.VMEM((rows, HD), F32),
            pltpu.VMEM((rows, HD), F32),
            pltpu.VMEM((3, heads, rows, HD), F32),
            pltpu.VMEM((3, rows, inner), BF),
            pltpu.VMEM((2, heads * SPLIT, deep, HD), F32),
            pltpu.VMEM((8, HD), F32),
            pltpu.VMEM((8, HD), F32),
            states, states, states, states, states,
            pltpu.VMEM((2, heads, HD, HD), BF),
            pltpu.VMEM((2, *piece), F32),
            pltpu.VMEM((2, *piece), F32),
            pltpu.VMEM((2, *piece), F32),
            pltpu.VMEM(piece, F32),
            pltpu.VMEM(piece, F32),
            dma((5 + heads,)),
            dma((2,)),
            dma((2, pieces)), dma((2, pieces)),
            dma((2, pieces)), dma((2, pieces)),
            dma((2, pieces)), dma((2, pieces)),
            dma((2, chunks)), dma((2, chunks)),
            dma((chunks,)), dma((chunks,)),
        ],
        compiler_params=pltpu.CompilerParams(
            collective_id=0, has_side_effects=True, vmem_limit_bytes=48 * 2**20
        ),
    )(*[pltpu.with_memory_space_constraint(x, pltpu.HBM) for x in operands])


def solution(mesh):
    nc, nt = mesh.shape["ctx"], mesh.shape["tp"]

    def local(tokens_in, w_query, w_key, w_value, grad_out, trajectory_ends):
        rows, width = tokens_in.shape
        heads = w_query.shape[1] // HD
        fits = nt == 4 and nc % 2 == 0 and heads % 2 == 0 and rows <= 512
        fits = fits and width % COLS == 0 and rows % 256 == 0
        call = functools.partial(fused_body, nc, nt) if fits else body
        return call(tokens_in, w_query, w_key, w_value, grad_out, trajectory_ends)

    return jax.shard_map(
        local,
        mesh=mesh,
        in_specs=(
            P("ctx", None),
            P(None, "tp"),
            P(None, "tp"),
            P(None, "tp"),
            P("ctx", "tp"),
            P("ctx"),
        ),
        out_specs=P(("ctx", "tp"), None),
        check_vma=False,
    )
```

```python
import functools

import jax
import jax.numpy as jnp
from jax import lax
from jax.experimental import pallas as pl
from jax.experimental.pallas import tpu as pltpu
from jax.sharding import PartitionSpec as P

HD = 128


def prefix(part, axis, combine, identity):
    count = lax.axis_size(axis)
    place = lax.axis_index(axis)
    ahead = count - 1 - place
    gathered = jax.tree.map(lambda a: lax.all_gather(a, axis), part)
    state = jax.tree.map(lambda a, e: jnp.zeros_like(a) + jnp.asarray(e, a.dtype), part, identity)

    def one(hop, state):
        source = count - 1 - hop
        return combine(
            state, jax.tree.map(lambda a: lax.dynamic_index_in_dim(a, source, 0, False), gathered)
        )

    return lax.fori_loop(0, ahead, one, state)


def joined(earlier, later):
    return (later[0] + (1.0 - later[1][0]) * earlier[0], jnp.maximum(earlier[1], later[1]))


def body(tokens_in, w_query, w_key, w_value, grad_out, trajectory_ends):
    row_count = tokens_in.shape[0]
    head_count = w_query.shape[1] // HD
    shape = (row_count, head_count, HD)
    queries = (
        jnp.dot(tokens_in, w_query, preferred_element_type=jnp.float32)
        .astype(jnp.bfloat16)
        .reshape(shape)
    )
    key_rows = (
        jnp.dot(tokens_in, w_key, preferred_element_type=jnp.float32)
        .astype(jnp.bfloat16)
        .reshape(shape)
    )
    value_rows = (
        jnp.dot(tokens_in, w_value, preferred_element_type=jnp.float32)
        .astype(jnp.bfloat16)
        .reshape(shape)
    )
    grad_rows = grad_out.reshape(shape)
    before = jnp.cumsum(trajectory_ends) - trajectory_ends
    end_total = jnp.sum(trajectory_ends)
    opened = before == 0
    closed = end_total - before == 0
    positions = jnp.arange(row_count, dtype=jnp.int32)
    pair_mask = (positions[None, :] <= positions[:, None]) & (before[:, None] == before[None, :])
    reset_any = (end_total > 0).astype(jnp.float32).reshape(1)
    open_bf = opened.astype(jnp.bfloat16)[:, None, None]
    close_bf = closed.astype(jnp.bfloat16)[:, None, None]
    carry_out = jnp.einsum(
        "shv,shk->hvk", value_rows * close_bf, key_rows, preferred_element_type=jnp.float32
    )
    grads_out = jnp.einsum(
        "thv,thk->hvk", grad_rows * open_bf, queries, preferred_element_type=jnp.float32
    )
    zero_state = jnp.zeros((head_count, HD, HD), jnp.float32)
    zero_flag = jnp.zeros((1,), jnp.float32)
    flag_list = lax.all_gather(reset_any, "ctx", axis=0, tiled=True)
    own_index = lax.axis_index("ctx")
    order = jnp.arange(flag_list.shape[0], dtype=jnp.int32)
    start_from = jnp.max(jnp.where((order < own_index) & (flag_list > 0), order, 0))
    piece = lax.all_gather(carry_out[None], "ctx", axis=0, tiled=True)
    index_list = jnp.arange(piece.shape[0], dtype=jnp.int32)
    weights = ((index_list >= start_from) & (index_list < own_index)).astype(jnp.float32)
    state_in = jnp.sum(weights[:, None, None, None] * piece, axis=0)
    grads_in = prefix((grads_out, reset_any), "ctx", joined, (zero_state, zero_flag))[0]
    scores = jnp.einsum("thv,shv->hts", grad_rows, value_rows, preferred_element_type=jnp.float32)
    scores = jnp.where(pair_mask[None], scores, 0.0).astype(jnp.bfloat16)
    attn = jnp.einsum("thk,shk->hts", queries, key_rows, preferred_element_type=jnp.float32)
    attn = jnp.where(pair_mask[None], attn, 0.0).astype(jnp.bfloat16)
    state_bf = state_in.astype(jnp.bfloat16)
    grads_bf = grads_in.astype(jnp.bfloat16)
    open_f = opened.astype(jnp.float32)[:, None, None]
    close_f = closed.astype(jnp.float32)[:, None, None]
    score_scale = 1.0 / HD
    grad_query = jnp.einsum("hts,shk->thk", scores, key_rows, preferred_element_type=jnp.float32)
    grad_query = grad_query + open_f * jnp.einsum(
        "thv,hvk->thk", grad_rows, state_bf, preferred_element_type=jnp.float32
    )
    grad_key = jnp.einsum("hts,thk->shk", scores, queries, preferred_element_type=jnp.float32)
    grad_key = grad_key + close_f * jnp.einsum(
        "shv,hvk->shk", value_rows, grads_bf, preferred_element_type=jnp.float32
    )
    grad_value = jnp.einsum("hts,thv->shv", attn, grad_rows, preferred_element_type=jnp.float32)
    grad_value = grad_value + close_f * jnp.einsum(
        "shk,hvk->shv", key_rows, grads_bf, preferred_element_type=jnp.float32
    )
    flat = (row_count, head_count * HD)
    grad_query = (score_scale * grad_query).astype(jnp.bfloat16).reshape(flat)
    grad_key = (score_scale * grad_key).astype(jnp.bfloat16).reshape(flat)
    grad_value = (score_scale * grad_value).astype(jnp.bfloat16).reshape(flat)
    dims = (((1,), (1,)), ((), ()))
    total = lax.dot_general(grad_query, w_query, dims, preferred_element_type=jnp.float32)
    total = total + lax.dot_general(grad_key, w_key, dims, preferred_element_type=jnp.float32)
    total = total + lax.dot_general(grad_value, w_value, dims, preferred_element_type=jnp.float32)
    shares = lax.psum_scatter(total, "tp", scatter_dimension=0, tiled=True)
    return shares.astype(jnp.bfloat16)


NN = ((1,), (0,))
NT = ((1,), (1,))
TN = ((0,), (0,))
COLS = 256
SPLIT = 2
BF = jnp.bfloat16
F32 = jnp.float32


def dot(a, b, dims):
    return lax.dot_general(a, b, (dims, ((), ())), preferred_element_type=F32)


def fused(
    nc, nt, tok_hbm, wq_hbm, wk_hbm, wv_hbm, g_hbm, ends_hbm, out_ref,
    ends_ref, tok, w, g, qkv, mask, flip, count, openc, closec, acc, dcat,
    st, fl, xfl, xr, cr, co, bs, br, fin,
    kept, sent, recd, ysent, yrecd,
    load_sem, fl_sem, x_send, x_recv, c_send, c_recv, b_send, b_recv,
    rs_send, rs_recv, y_send, y_recv,
):
    rows, width = tok.shape
    heads = g.shape[0]
    inner = w.shape[2]
    half = heads // 2
    pieces = half * SPLIT
    deep = HD // SPLIT
    chunks = width // COLS
    share = rows // nt
    ctx = lax.axis_index("ctx")
    tp = lax.axis_index("tp")
    par, pair = ctx % 2, ctx // 2
    pairs = nc // 2
    lo, hi = tp % 2, tp // 2
    mate = ctx + 1 - 2 * par
    core = tp + 1 - 2 * lo
    over = tp + 2 - 4 * hi

    turn = jnp.where(pair >= pairs // 2, 1, 0)
    block = rows // 2
    token_loads = [
        pltpu.make_async_copy(tok_hbm.at[at, :], tok.at[at, :], load_sem.at[n])
        for n, at in enumerate((slice(0, block), slice(block, rows)))
    ]
    sides = inner // COLS

    def weight_load(ref, which, side):
        at = pl.ds(pl.multiple_of(side * COLS, COLS), COLS)
        return pltpu.make_async_copy(
            ref.at[:, at], w.at[which, :, at], load_sem.at[3 + heads + which * sides + side]
        )

    def start_weight(ref, which):
        for side in range(sides):
            weight_load(ref, which, side).start()

    g_loads = [
        pltpu.make_async_copy(g_hbm.at[:, pl.ds(h * HD, HD)], g.at[h], load_sem.at[2 + h])
        for h in range(heads)
    ]
    ends_load = pltpu.make_async_copy(ends_hbm, ends_ref, load_sem.at[2 + heads])
    ends_load.start()
    for load in token_loads:
        load.start()

    @pl.when(turn == 1)
    def _():
        start_weight(wq_hbm, 0)
        for load in g_loads:
            load.start()

    start_weight(wk_hbm, 1)
    start_weight(wv_hbm, 2)

    @pl.when(turn == 0)
    def _():
        start_weight(wq_hbm, 0)
        for load in g_loads:
            load.start()

    barrier = pltpu.get_barrier_semaphore()
    pl.semaphore_signal(barrier, inc=1, device_id={"ctx": mate}, device_id_type=pl.DeviceIdType.MESH)
    pl.semaphore_signal(barrier, inc=1, device_id={"tp": core}, device_id_type=pl.DeviceIdType.MESH)
    pl.semaphore_signal(barrier, inc=1, device_id={"tp": over}, device_id_type=pl.DeviceIdType.MESH)

    @pl.when(pair > 0)
    def _():
        pl.semaphore_signal(
            barrier, inc=1, device_id={"ctx": ctx - 2}, device_id_type=pl.DeviceIdType.MESH
        )

    @pl.when(pair < pairs - 1)
    def _():
        pl.semaphore_signal(
            barrier, inc=1, device_id={"ctx": ctx + 2}, device_id_type=pl.DeviceIdType.MESH
        )

    def remote(src, dst, send, recv, device):
        return pltpu.make_async_remote_copy(
            src_ref=src, dst_ref=dst, send_sem=send, recv_sem=recv,
            device_id=device, device_id_type=pl.DeviceIdType.MESH,
        )

    ends_load.wait()
    ends_row = jnp.broadcast_to(ends_ref[...].astype(F32), (HD, rows)).astype(BF)
    row_id = lax.broadcasted_iota(jnp.int32, (rows, rows), 0)
    col_id = lax.broadcasted_iota(jnp.int32, (rows, rows), 1)
    above = (col_id < row_id).astype(F32).astype(BF)
    before_col = dot(above, ends_row, NT)
    total = jnp.sum(ends_ref[...].astype(F32), axis=1, keepdims=True)
    count[...] = before_col
    openc[...] = (before_col == 0.0).astype(F32)
    closec[...] = (jnp.broadcast_to(total, (rows, HD)) == before_col).astype(F32)
    fl[...] = jnp.broadcast_to((total > 0.0).astype(F32), fl.shape)

    spans = [(0, block), (block, rows)]
    per_side = COLS // HD

    def project(which, side):
        at = pl.ds(pl.multiple_of(side * COLS, COLS), COLS)
        weight_load(wk_hbm, which, side).wait()
        made = dot(tok[...], w[which, :, at], NN).astype(BF)
        for n in range(per_side):
            qkv[which, side * per_side + n] = made[:, n * HD : (n + 1) * HD]

    def x_copy(d, i):
        return remote(
            st.at[d, (1 - par) * pieces + i], xr.at[d, i],
            x_send.at[d, i], x_recv.at[d, i], {"ctx": mate},
        )

    def state(d, h):
        def hold(made):
            for n in range(SPLIT):
                st[d, h * SPLIT + n] = made[n * deep : (n + 1) * deep]

        @pl.when(d == 0)
        def _():
            hold(dot(qkv[2, h] * closec[...].astype(BF), qkv[1, h], TN))

        @pl.when(d == 1)
        def _():
            hold(dot(g[h] * openc[...].astype(BF), qkv[0, h], TN))

    def give(d):
        @pl.loop(0, half)
        def _(i):
            state(d, (1 - par) * half + i)
            for n in range(SPLIT):
                x_copy(d, i * SPLIT + n).start()

    for load in token_loads:
        load.wait()

    @pl.loop(0, (2 - turn) * sides)
    def _(n):
        project(jnp.where(turn == 0, 1 + n // sides, 0), n % sides)

    for load in g_loads:
        load.wait()
    waits = 3 + jnp.where(pair > 0, 1, 0) + jnp.where(pair < pairs - 1, 1, 0)
    pl.semaphore_wait(barrier, waits)
    flag_copy = remote(fl, xfl, fl_sem.at[0], fl_sem.at[1], {"ctx": mate})
    flag_copy.start()
    give(turn)

    @pl.loop(0, (1 + turn) * sides)
    def _(n):
        project(jnp.where(turn == 0, 0, 1 + n // sides), n % sides)

    give(1 - turn)

    @pl.loop(0, 2 * half)
    def _(n):
        state((n // half + turn) % 2, par * half + n % half)

    below = (row_id < col_id).astype(F32).astype(BF)
    before_row = dot(ends_row, below, NN)[0:1, :]
    same = before_row == jnp.broadcast_to(count[:, 0:1], (rows, rows))
    mask[...] = (same & (col_id <= row_id)).astype(F32).astype(BF)
    flip[...] = (same & (row_id <= col_id)).astype(F32).astype(BF)

    def within(h):
        for start, stop in spans:
            at, upto, onward = slice(start, stop), slice(0, stop), slice(start, rows)
            scores = dot(g[h, at, :], qkv[2, h, upto, :], NT).astype(BF) * mask[at, upto]
            acc[0, h, at, :] = dot(scores, qkv[1, h, upto, :], NN)
            turned = dot(qkv[2, h, at, :], g[h, onward, :], NT).astype(BF) * flip[at, onward]
            acc[1, h, at, :] = dot(turned, qkv[0, h, onward, :], NN)
            attn = dot(qkv[1, h, at, :], qkv[0, h, onward, :], NT).astype(BF) * flip[at, onward]
            acc[2, h, at, :] = dot(attn, g[h, onward, :], NN)

    def within_some(first, last):
        @pl.loop(first, last)
        def _(h):
            within(h)

    def c_copy(d, i):
        return remote(
            co.at[d, i], cr.at[d, i], c_send.at[d, i], c_recv.at[d, i],
            {"ctx": ctx + 2 - 4 * d},
        )

    def b_copy(d, i):
        return remote(bs.at[d, i], br.at[d, i], b_send.at[d, i], b_recv.at[d, i], {"ctx": mate})

    def has_next(d):
        return ((d == 0) & (pair < pairs - 1)) | ((d == 1) & (pair > 0))

    def has_prev(d):
        return ((d == 0) & (pair > 0)) | ((d == 1) & (pair < pairs - 1))

    def place(i):
        return slice(i % SPLIT * deep, (i % SPLIT + 1) * deep)

    def carry(d):
        first_here = par == d
        more, begun = has_next(d), has_prev(d)
        own_flag, mate_flag = fl[0:1, :], xfl[0:1, :]
        first_flag = jnp.where(first_here, own_flag, mate_flag)
        second_flag = jnp.where(first_here, mate_flag, own_flag)

        @pl.when(jnp.logical_not(begun))
        def _():
            cr[d] = jnp.zeros(cr.shape[1:], F32)

        for i in range(pieces):
            x_copy(d, i).wait_recv()
            own, other = st[d, par * pieces + i], xr[d, i]
            first = jnp.where(first_here, own, other)
            second = jnp.where(first_here, other, own)

            @pl.when(begun)
            def _():
                c_copy(d, i).wait_recv()

            into = cr[d, i]
            inner = first + (1.0 - first_flag) * into

            @pl.when(more)
            def _():
                co[d, i] = second + (1.0 - second_flag) * inner
                c_copy(d, i).start()

            bs[d, i] = jnp.where(first_here, inner, into)
            b_copy(d, i).start()
            mine = jnp.where(first_here, into, inner).astype(BF)
            fin[d, par * half + i // SPLIT, place(i), :] = mine

    at_end = (pair == 0) | (pair == pairs - 1)
    early = jnp.where(at_end, 0, heads // 4)
    late = jnp.where(at_end, heads - heads // 4, heads // 2)
    flag_copy.wait_recv()
    within_some(0, early)
    carry(turn)
    within_some(early, late)
    carry(1 - turn)
    within_some(late, heads)

    scale = 1.0 / HD

    def finish(d, h):
        at = pl.ds(pl.multiple_of(h * HD, HD), HD)

        @pl.when(d == 0)
        def _():
            dq = acc[0, h] + openc[...] * dot(g[h], fin[0, h], NN)
            dcat[0, :, at] = (scale * dq).astype(BF)

        @pl.when(d == 1)
        def _():
            b_in, closed = fin[1, h], closec[...]
            dk = acc[1, h] + closed * dot(qkv[2, h], b_in, NN)
            dv = acc[2, h] + closed * dot(qkv[1, h], b_in, NT)
            dcat[1, :, at] = (scale * dk).astype(BF)
            dcat[2, :, at] = (scale * dv).astype(BF)

    @pl.loop(0, 2 * half)
    def _(n):
        finish((n // half + turn) % 2, par * half + n % half)

    for d in (turn, 1 - turn):
        for i in range(half):
            h = (1 - par) * half + i
            for n in range(i * SPLIT, (i + 1) * SPLIT):
                b_copy(d, n).wait_recv()
                fin[d, h, place(n), :] = br[d, n].astype(BF)
            finish(d, h)

    def rs_copy(part, j):
        return remote(
            sent.at[part, j], recd.at[part, j], rs_send.at[part, j], rs_recv.at[part, j],
            {"tp": core},
        )

    def y_copy(j):
        return remote(ysent.at[j], yrecd.at[j], y_send.at[j], y_recv.at[j], {"tp": over})

    def product(part, j):
        side = jnp.where(part == 0, 1 - hi, hi)
        at = pl.ds(pl.multiple_of(side * 2 * share, 2 * share), 2 * share)
        cols = pl.ds(pl.multiple_of(j * COLS, COLS), COLS)
        made = dot(dcat[0, at, :], w[0, cols, :], NT)
        made = made + dot(dcat[1, at, :], w[1, cols, :], NT)
        made = made + dot(dcat[2, at, :], w[2, cols, :], NT)
        low, high = made[0:share], made[share : 2 * share]
        sent[part, j] = jnp.where(lo == 0, high, low)
        kept[part, j] = jnp.where(lo == 0, low, high)
        rs_copy(part, j).start()

    def pass_on(j):
        rs_copy(0, j).wait_recv()
        ysent[j] = kept[0, j] + recd[0, j]
        y_copy(j).start()

    product(0, 0)

    @pl.loop(1, chunks)
    def _(j):
        product(0, j)
        pass_on(j - 1)

    product(1, 0)
    pass_on(chunks - 1)

    @pl.loop(1, chunks)
    def _(j):
        product(1, j)

    for j in range(chunks):
        rs_copy(1, j).wait_recv()
        y_copy(j).wait_recv()
        out_ref[:, j * COLS : (j + 1) * COLS] = (kept[1, j] + recd[1, j] + yrecd[j]).astype(BF)

    flag_copy.wait_send()
    for d in range(2):
        for i in range(pieces):
            x_copy(d, i).wait_send()
            b_copy(d, i).wait_send()

        @pl.when(has_next(d))
        def _():
            for i in range(pieces):
                c_copy(d, i).wait_send()

    @pl.loop(0, chunks)
    def _(j):
        rs_copy(0, j).wait_send()
        rs_copy(1, j).wait_send()
        y_copy(j).wait_send()


def fused_body(nc, nt, tokens_in, w_query, w_key, w_value, grad_out, trajectory_ends):
    rows, width = tokens_in.shape
    inner = w_query.shape[1]
    heads = inner // HD
    half = heads // 2
    share = rows // nt
    chunks = width // COLS
    outside = pl.BlockSpec(memory_space=pltpu.HBM)
    vmem = pl.BlockSpec(memory_space=pltpu.VMEM)
    dma = pltpu.SemaphoreType.DMA
    pieces = half * SPLIT
    deep = HD // SPLIT
    states = pltpu.VMEM((2, pieces, deep, HD), F32)
    piece = (chunks, share, COLS)
    operands = (tokens_in, w_query, w_key, w_value, grad_out, trajectory_ends.reshape(1, rows))
    return pl.pallas_call(
        functools.partial(fused, nc, nt),
        out_shape=jax.ShapeDtypeStruct((share, width), BF),
        in_specs=[outside] * 6,
        out_specs=vmem,
        scratch_shapes=[
            pltpu.VMEM((1, rows), jnp.int32),
            pltpu.VMEM((rows, width), BF),
            pltpu.VMEM((3, width, inner), BF),
            pltpu.VMEM((heads, rows, HD), BF),
            pltpu.VMEM((3, heads, rows, HD), BF),
            pltpu.VMEM((rows, rows), BF),
            pltpu.VMEM((rows, rows), BF),
            pltpu.VMEM((rows, HD), F32),
            pltpu.VMEM((rows, HD), F32),
            pltpu.VMEM((rows, HD), F32),
            pltpu.VMEM((3, heads, rows, HD), F32),
            pltpu.VMEM((3, rows, inner), BF),
            pltpu.VMEM((2, heads * SPLIT, deep, HD), F32),
            pltpu.VMEM((8, HD), F32),
            pltpu.VMEM((8, HD), F32),
            states, states, states, states, states,
            pltpu.VMEM((2, heads, HD, HD), BF),
            pltpu.VMEM((2, *piece), F32),
            pltpu.VMEM((2, *piece), F32),
            pltpu.VMEM((2, *piece), F32),
            pltpu.VMEM(piece, F32),
            pltpu.VMEM(piece, F32),
            dma((3 + heads + 3 * (inner // COLS),)),
            dma((2,)),
            dma((2, pieces)), dma((2, pieces)),
            dma((2, pieces)), dma((2, pieces)),
            dma((2, pieces)), dma((2, pieces)),
            dma((2, chunks)), dma((2, chunks)),
            dma((chunks,)), dma((chunks,)),
        ],
        compiler_params=pltpu.CompilerParams(
            collective_id=0, has_side_effects=True, vmem_limit_bytes=48 * 2**20
        ),
    )(*[pltpu.with_memory_space_constraint(x, pltpu.HBM) for x in operands])


def solution(mesh):
    nc, nt = mesh.shape["ctx"], mesh.shape["tp"]

    def local(tokens_in, w_query, w_key, w_value, grad_out, trajectory_ends):
        rows, width = tokens_in.shape
        heads = w_query.shape[1] // HD
        fits = nt == 4 and nc % 2 == 0 and heads % 2 == 0 and rows <= 512
        fits = fits and width % COLS == 0 and rows % 256 == 0 and w_query.shape[1] % COLS == 0
        call = functools.partial(fused_body, nc, nt) if fits else body
        return call(tokens_in, w_query, w_key, w_value, grad_out, trajectory_ends)

    return jax.shard_map(
        local,
        mesh=mesh,
        in_specs=(
            P("ctx", None),
            P(None, "tp"),
            P(None, "tp"),
            P(None, "tp"),
            P("ctx", "tp"),
            P("ctx"),
        ),
        out_specs=P(("ctx", "tp"), None),
        check_vma=False,
    )
```

```python
import functools

import jax
import jax.numpy as jnp
from jax import lax
from jax.experimental import pallas as pl
from jax.experimental.pallas import tpu as pltpu
from jax.sharding import PartitionSpec as P

HD = 128


def prefix(part, axis, combine, identity):
    count = lax.axis_size(axis)
    place = lax.axis_index(axis)
    ahead = count - 1 - place
    gathered = jax.tree.map(lambda a: lax.all_gather(a, axis), part)
    state = jax.tree.map(lambda a, e: jnp.zeros_like(a) + jnp.asarray(e, a.dtype), part, identity)

    def one(hop, state):
        source = count - 1 - hop
        return combine(
            state, jax.tree.map(lambda a: lax.dynamic_index_in_dim(a, source, 0, False), gathered)
        )

    return lax.fori_loop(0, ahead, one, state)


def joined(earlier, later):
    return (later[0] + (1.0 - later[1][0]) * earlier[0], jnp.maximum(earlier[1], later[1]))


def body(tokens_in, w_query, w_key, w_value, grad_out, trajectory_ends):
    row_count = tokens_in.shape[0]
    head_count = w_query.shape[1] // HD
    shape = (row_count, head_count, HD)
    queries = (
        jnp.dot(tokens_in, w_query, preferred_element_type=jnp.float32)
        .astype(jnp.bfloat16)
        .reshape(shape)
    )
    key_rows = (
        jnp.dot(tokens_in, w_key, preferred_element_type=jnp.float32)
        .astype(jnp.bfloat16)
        .reshape(shape)
    )
    value_rows = (
        jnp.dot(tokens_in, w_value, preferred_element_type=jnp.float32)
        .astype(jnp.bfloat16)
        .reshape(shape)
    )
    grad_rows = grad_out.reshape(shape)
    before = jnp.cumsum(trajectory_ends) - trajectory_ends
    end_total = jnp.sum(trajectory_ends)
    opened = before == 0
    closed = end_total - before == 0
    positions = jnp.arange(row_count, dtype=jnp.int32)
    pair_mask = (positions[None, :] <= positions[:, None]) & (before[:, None] == before[None, :])
    reset_any = (end_total > 0).astype(jnp.float32).reshape(1)
    open_bf = opened.astype(jnp.bfloat16)[:, None, None]
    close_bf = closed.astype(jnp.bfloat16)[:, None, None]
    carry_out = jnp.einsum(
        "shv,shk->hvk", value_rows * close_bf, key_rows, preferred_element_type=jnp.float32
    )
    grads_out = jnp.einsum(
        "thv,thk->hvk", grad_rows * open_bf, queries, preferred_element_type=jnp.float32
    )
    zero_state = jnp.zeros((head_count, HD, HD), jnp.float32)
    zero_flag = jnp.zeros((1,), jnp.float32)
    flag_list = lax.all_gather(reset_any, "ctx", axis=0, tiled=True)
    own_index = lax.axis_index("ctx")
    order = jnp.arange(flag_list.shape[0], dtype=jnp.int32)
    start_from = jnp.max(jnp.where((order < own_index) & (flag_list > 0), order, 0))
    piece = lax.all_gather(carry_out[None], "ctx", axis=0, tiled=True)
    index_list = jnp.arange(piece.shape[0], dtype=jnp.int32)
    weights = ((index_list >= start_from) & (index_list < own_index)).astype(jnp.float32)
    state_in = jnp.sum(weights[:, None, None, None] * piece, axis=0)
    grads_in = prefix((grads_out, reset_any), "ctx", joined, (zero_state, zero_flag))[0]
    scores = jnp.einsum("thv,shv->hts", grad_rows, value_rows, preferred_element_type=jnp.float32)
    scores = jnp.where(pair_mask[None], scores, 0.0).astype(jnp.bfloat16)
    attn = jnp.einsum("thk,shk->hts", queries, key_rows, preferred_element_type=jnp.float32)
    attn = jnp.where(pair_mask[None], attn, 0.0).astype(jnp.bfloat16)
    state_bf = state_in.astype(jnp.bfloat16)
    grads_bf = grads_in.astype(jnp.bfloat16)
    open_f = opened.astype(jnp.float32)[:, None, None]
    close_f = closed.astype(jnp.float32)[:, None, None]
    score_scale = 1.0 / HD
    grad_query = jnp.einsum("hts,shk->thk", scores, key_rows, preferred_element_type=jnp.float32)
    grad_query = grad_query + open_f * jnp.einsum(
        "thv,hvk->thk", grad_rows, state_bf, preferred_element_type=jnp.float32
    )
    grad_key = jnp.einsum("hts,thk->shk", scores, queries, preferred_element_type=jnp.float32)
    grad_key = grad_key + close_f * jnp.einsum(
        "shv,hvk->shk", value_rows, grads_bf, preferred_element_type=jnp.float32
    )
    grad_value = jnp.einsum("hts,thv->shv", attn, grad_rows, preferred_element_type=jnp.float32)
    grad_value = grad_value + close_f * jnp.einsum(
        "shk,hvk->shv", key_rows, grads_bf, preferred_element_type=jnp.float32
    )
    flat = (row_count, head_count * HD)
    grad_query = (score_scale * grad_query).astype(jnp.bfloat16).reshape(flat)
    grad_key = (score_scale * grad_key).astype(jnp.bfloat16).reshape(flat)
    grad_value = (score_scale * grad_value).astype(jnp.bfloat16).reshape(flat)
    dims = (((1,), (1,)), ((), ()))
    total = lax.dot_general(grad_query, w_query, dims, preferred_element_type=jnp.float32)
    total = total + lax.dot_general(grad_key, w_key, dims, preferred_element_type=jnp.float32)
    total = total + lax.dot_general(grad_value, w_value, dims, preferred_element_type=jnp.float32)
    shares = lax.psum_scatter(total, "tp", scatter_dimension=0, tiled=True)
    return shares.astype(jnp.bfloat16)


NN = ((1,), (0,))
NT = ((1,), (1,))
TN = ((0,), (0,))
COLS = 256
SPLIT = 4
BF = jnp.bfloat16
F32 = jnp.float32


def dot(a, b, dims):
    return lax.dot_general(a, b, (dims, ((), ())), preferred_element_type=F32)


def fused(
    nc, nt, tok_hbm, wq_hbm, wk_hbm, wv_hbm, g_hbm, ends_hbm, out_ref,
    ends_ref, tok, w, g, qkv, mask, flip, openc, closec, acc, dcat,
    st, fl, xfl, xr, cr, co, bs, br, fin,
    kept, sent, recd, ysent, yrecd,
    load_sem, fl_sem, x_send, x_recv, c_send, c_recv, b_send, b_recv,
    rs_send, rs_recv, y_send, y_recv,
):
    rows, width = tok.shape
    heads = g.shape[0]
    half = heads // 2
    pieces = half * SPLIT
    deep = HD // SPLIT
    chunks = width // COLS
    share = rows // nt
    ctx = lax.axis_index("ctx")
    tp = lax.axis_index("tp")
    par, pair = ctx % 2, ctx // 2
    pairs = nc // 2
    lo, hi = tp % 2, tp // 2
    mate = ctx + 1 - 2 * par
    core = tp + 1 - 2 * lo
    over = tp + 2 - 4 * hi

    turn = jnp.where(pair >= pairs // 2, 1, 0)
    token_load = pltpu.make_async_copy(tok_hbm, tok, load_sem.at[0])
    weight_loads = [
        pltpu.make_async_copy(ref, w.at[n], load_sem.at[1 + n])
        for n, ref in enumerate((wq_hbm, wk_hbm, wv_hbm))
    ]
    g_loads = [
        pltpu.make_async_copy(g_hbm.at[:, pl.ds(h * HD, HD)], g.at[h], load_sem.at[4 + h])
        for h in range(heads)
    ]
    ends_load = pltpu.make_async_copy(ends_hbm, ends_ref, load_sem.at[4 + heads])
    ends_load.start()
    token_load.start()

    @pl.when(turn == 0)
    def _():
        for n in (1, 2, 0):
            weight_loads[n].start()
        for load in g_loads:
            load.start()

    @pl.when(turn == 1)
    def _():
        weight_loads[0].start()
        for load in g_loads:
            load.start()
        for n in (1, 2):
            weight_loads[n].start()

    barrier = pltpu.get_barrier_semaphore()
    pl.semaphore_signal(barrier, inc=1, device_id={"ctx": mate}, device_id_type=pl.DeviceIdType.MESH)
    pl.semaphore_signal(barrier, inc=1, device_id={"tp": core}, device_id_type=pl.DeviceIdType.MESH)
    pl.semaphore_signal(barrier, inc=1, device_id={"tp": over}, device_id_type=pl.DeviceIdType.MESH)

    @pl.when(pair > 0)
    def _():
        pl.semaphore_signal(
            barrier, inc=1, device_id={"ctx": ctx - 2}, device_id_type=pl.DeviceIdType.MESH
        )

    @pl.when(pair < pairs - 1)
    def _():
        pl.semaphore_signal(
            barrier, inc=1, device_id={"ctx": ctx + 2}, device_id_type=pl.DeviceIdType.MESH
        )

    def remote(src, dst, send, recv, device):
        return pltpu.make_async_remote_copy(
            src_ref=src, dst_ref=dst, send_sem=send, recv_sem=recv,
            device_id=device, device_id_type=pl.DeviceIdType.MESH,
        )

    ends_load.wait()
    ends_row = jnp.broadcast_to(ends_ref[...].astype(F32), (HD, rows)).astype(BF)
    row_id = lax.broadcasted_iota(jnp.int32, (rows, rows), 0)
    col_id = lax.broadcasted_iota(jnp.int32, (rows, rows), 1)
    below = (row_id < col_id).astype(F32).astype(BF)
    above = (col_id < row_id).astype(F32).astype(BF)
    before_row = dot(ends_row, below, NN)[0:1, :]
    before_col = dot(above, ends_row, NT)
    total = jnp.sum(ends_ref[...].astype(F32), axis=1, keepdims=True)
    openc[...] = (before_col == 0.0).astype(F32)
    closec[...] = (jnp.broadcast_to(total, (rows, HD)) == before_col).astype(F32)
    fl[...] = jnp.broadcast_to((total > 0.0).astype(F32), fl.shape)
    same = before_row == jnp.broadcast_to(before_col[:, 0:1], (rows, rows))
    mask[...] = (same & (col_id <= row_id)).astype(F32).astype(BF)
    flip[...] = (same & (row_id <= col_id)).astype(F32).astype(BF)

    block = min(256, rows)
    spans = [(at, at + block) for at in range(0, rows, block)]

    def project(which):
        @pl.loop(0, rows // block)
        def _(step):
            at = pl.ds(pl.multiple_of(step * block, block), block)
            made = dot(tok[at, :], w[which], NN).astype(BF)
            for h in range(heads):
                qkv[which, h, at, :] = made[:, h * HD : (h + 1) * HD]

    def x_copy(d, i):
        return remote(
            st.at[d, (1 - par) * pieces + i], xr.at[d, i],
            x_send.at[d, i], x_recv.at[d, i], {"ctx": mate},
        )

    def state(d, h):
        if d == 0:
            made = dot(qkv[2, h] * closec[...].astype(BF), qkv[1, h], TN)
        else:
            made = dot(g[h] * openc[...].astype(BF), qkv[0, h], TN)
        for n in range(SPLIT):
            st[d, h * SPLIT + n] = made[n * deep : (n + 1) * deep]

    def give(d):
        for i in range(half):
            state(d, (1 - par) * half + i)
            for n in range(SPLIT):
                x_copy(d, i * SPLIT + n).start()

    def keys_values():
        for n in (1, 2):
            weight_loads[n].wait()
            project(n)

    def queries():
        weight_loads[0].wait()
        project(0)

    token_load.wait()

    @pl.when(turn == 0)
    def _():
        keys_values()

    @pl.when(turn == 1)
    def _():
        queries()

    for load in g_loads:
        load.wait()
    waits = 3 + jnp.where(pair > 0, 1, 0) + jnp.where(pair < pairs - 1, 1, 0)
    pl.semaphore_wait(barrier, waits)
    flag_copy = remote(fl, xfl, fl_sem.at[0], fl_sem.at[1], {"ctx": mate})
    flag_copy.start()

    @pl.when(turn == 0)
    def _():
        give(0)
        queries()
        give(1)

    @pl.when(turn == 1)
    def _():
        give(1)
        keys_values()
        give(0)

    for i in range(half):
        state(0, par * half + i)
        state(1, par * half + i)

    def within(h):
        for start, stop in spans:
            at, upto, onward = slice(start, stop), slice(0, stop), slice(start, rows)
            scores = dot(g[h, at, :], qkv[2, h, upto, :], NT).astype(BF) * mask[at, upto]
            acc[0, h, at, :] = dot(scores, qkv[1, h, upto, :], NN)
            turned = dot(qkv[2, h, at, :], g[h, onward, :], NT).astype(BF) * flip[at, onward]
            acc[1, h, at, :] = dot(turned, qkv[0, h, onward, :], NN)
            attn = dot(qkv[1, h, at, :], qkv[0, h, onward, :], NT).astype(BF) * flip[at, onward]
            acc[2, h, at, :] = dot(attn, g[h, onward, :], NN)

    def within_some(first, last):
        @pl.loop(first, last)
        def _(h):
            within(h)

    def c_copy(d, i):
        return remote(
            co.at[d, i], cr.at[d, i], c_send.at[d, i], c_recv.at[d, i],
            {"ctx": ctx + 2 - 4 * d},
        )

    def b_copy(d, i):
        return remote(bs.at[d, i], br.at[d, i], b_send.at[d, i], b_recv.at[d, i], {"ctx": mate})

    def has_next(d):
        return ((d == 0) & (pair < pairs - 1)) | ((d == 1) & (pair > 0))

    def has_prev(d):
        return ((d == 0) & (pair > 0)) | ((d == 1) & (pair < pairs - 1))

    def place(i):
        return slice(i % SPLIT * deep, (i % SPLIT + 1) * deep)

    def carry(d):
        first_here = par == d
        more, begun = has_next(d), has_prev(d)
        own_flag, mate_flag = fl[0:1, :], xfl[0:1, :]
        first_flag = jnp.where(first_here, own_flag, mate_flag)
        second_flag = jnp.where(first_here, mate_flag, own_flag)

        @pl.when(jnp.logical_not(begun))
        def _():
            cr[d] = jnp.zeros(cr.shape[1:], F32)

        for i in range(pieces):
            x_copy(d, i).wait_recv()
            own, other = st[d, par * pieces + i], xr[d, i]
            first = jnp.where(first_here, own, other)
            second = jnp.where(first_here, other, own)

            @pl.when(begun)
            def _():
                c_copy(d, i).wait_recv()

            into = cr[d, i]
            inner = first + (1.0 - first_flag) * into

            @pl.when(more)
            def _():
                co[d, i] = second + (1.0 - second_flag) * inner
                c_copy(d, i).start()

            bs[d, i] = jnp.where(first_here, inner, into)
            b_copy(d, i).start()
            mine = jnp.where(first_here, into, inner).astype(BF)
            fin[d, par * half + i // SPLIT, place(i), :] = mine

    scale = 1.0 / HD

    def finish(d, h):
        at = pl.ds(pl.multiple_of(h * HD, HD), HD)

        @pl.when(d == 0)
        def _():
            dq = acc[0, h] + openc[...] * dot(g[h], fin[0, h], NN)
            dcat[0, :, at] = (scale * dq).astype(BF)

        @pl.when(d == 1)
        def _():
            b_in, closed = fin[1, h], closec[...]
            dk = acc[1, h] + closed * dot(qkv[2, h], b_in, NN)
            dv = acc[2, h] + closed * dot(qkv[1, h], b_in, NT)
            dcat[1, :, at] = (scale * dk).astype(BF)
            dcat[2, :, at] = (scale * dv).astype(BF)

    def finish_own(d):
        @pl.loop(0, half)
        def _(i):
            finish(d, par * half + i)

    def finish_mate(d):
        @pl.loop(0, half)
        def _(i):
            h = (1 - par) * half + i
            for n in range(SPLIT):
                b_copy(d, i * SPLIT + n).wait_recv()
                fin[d, h, place(n), :] = br[d, i * SPLIT + n].astype(BF)
            finish(d, h)

    at_end = (pair == 0) | (pair == pairs - 1)
    early = jnp.where(at_end, 0, heads // 4)
    late = jnp.where(at_end, heads, heads // 2)
    flag_copy.wait_recv()
    within_some(0, early)
    carry(turn)
    within_some(early, late)

    @pl.when(at_end)
    def _():
        finish_own(turn)
        finish_mate(turn)

    carry(1 - turn)
    within_some(late, heads)

    @pl.when(jnp.logical_not(at_end))
    def _():
        finish_own(turn)
        finish_mate(turn)

    finish_own(1 - turn)
    finish_mate(1 - turn)

    def rs_copy(part, j):
        return remote(
            sent.at[part, j], recd.at[part, j], rs_send.at[part, j], rs_recv.at[part, j],
            {"tp": core},
        )

    def y_copy(j):
        return remote(ysent.at[j], yrecd.at[j], y_send.at[j], y_recv.at[j], {"tp": over})

    def product(part, j):
        side = jnp.where(part == 0, 1 - hi, hi)
        at = pl.ds(pl.multiple_of(side * 2 * share, 2 * share), 2 * share)
        cols = pl.ds(pl.multiple_of(j * COLS, COLS), COLS)
        made = dot(dcat[0, at, :], w[0, cols, :], NT)
        made = made + dot(dcat[1, at, :], w[1, cols, :], NT)
        made = made + dot(dcat[2, at, :], w[2, cols, :], NT)
        low, high = made[0:share], made[share : 2 * share]
        sent[part, j] = jnp.where(lo == 0, high, low)
        kept[part, j] = jnp.where(lo == 0, low, high)
        rs_copy(part, j).start()

    def pass_on(j):
        rs_copy(0, j).wait_recv()
        ysent[j] = kept[0, j] + recd[0, j]
        y_copy(j).start()

    product(0, 0)

    @pl.loop(1, chunks)
    def _(j):
        product(0, j)
        pass_on(j - 1)

    product(1, 0)
    pass_on(chunks - 1)

    @pl.loop(1, chunks)
    def _(j):
        product(1, j)

    for j in range(chunks):
        rs_copy(1, j).wait_recv()
        y_copy(j).wait_recv()
        out_ref[:, j * COLS : (j + 1) * COLS] = (kept[1, j] + recd[1, j] + yrecd[j]).astype(BF)

    flag_copy.wait_send()
    for d in range(2):
        for i in range(pieces):
            x_copy(d, i).wait_send()
            b_copy(d, i).wait_send()

        @pl.when(has_next(d))
        def _():
            for i in range(pieces):
                c_copy(d, i).wait_send()

    @pl.loop(0, chunks)
    def _(j):
        rs_copy(0, j).wait_send()
        rs_copy(1, j).wait_send()
        y_copy(j).wait_send()


def fused_body(nc, nt, tokens_in, w_query, w_key, w_value, grad_out, trajectory_ends):
    rows, width = tokens_in.shape
    inner = w_query.shape[1]
    heads = inner // HD
    half = heads // 2
    share = rows // nt
    chunks = width // COLS
    outside = pl.BlockSpec(memory_space=pltpu.HBM)
    vmem = pl.BlockSpec(memory_space=pltpu.VMEM)
    dma = pltpu.SemaphoreType.DMA
    pieces = half * SPLIT
    deep = HD // SPLIT
    states = pltpu.VMEM((2, pieces, deep, HD), F32)
    piece = (chunks, share, COLS)
    operands = (tokens_in, w_query, w_key, w_value, grad_out, trajectory_ends.reshape(1, rows))
    return pl.pallas_call(
        functools.partial(fused, nc, nt),
        out_shape=jax.ShapeDtypeStruct((share, width), BF),
        in_specs=[outside] * 6,
        out_specs=vmem,
        scratch_shapes=[
            pltpu.VMEM((1, rows), jnp.int32),
            pltpu.VMEM((rows, width), BF),
            pltpu.VMEM((3, width, inner), BF),
            pltpu.VMEM((heads, rows, HD), BF),
            pltpu.VMEM((3, heads, rows, HD), BF),
            pltpu.VMEM((rows, rows), BF),
            pltpu.VMEM((rows, rows), BF),
            pltpu.VMEM((rows, HD), F32),
            pltpu.VMEM((rows, HD), F32),
            pltpu.VMEM((3, heads, rows, HD), F32),
            pltpu.VMEM((3, rows, inner), BF),
            pltpu.VMEM((2, heads * SPLIT, deep, HD), F32),
            pltpu.VMEM((8, HD), F32),
            pltpu.VMEM((8, HD), F32),
            states, states, states, states, states,
            pltpu.VMEM((2, heads, HD, HD), BF),
            pltpu.VMEM((2, *piece), F32),
            pltpu.VMEM((2, *piece), F32),
            pltpu.VMEM((2, *piece), F32),
            pltpu.VMEM(piece, F32),
            pltpu.VMEM(piece, F32),
            dma((5 + heads,)),
            dma((2,)),
            dma((2, pieces)), dma((2, pieces)),
            dma((2, pieces)), dma((2, pieces)),
            dma((2, pieces)), dma((2, pieces)),
            dma((2, chunks)), dma((2, chunks)),
            dma((chunks,)), dma((chunks,)),
        ],
        compiler_params=pltpu.CompilerParams(
            collective_id=0, has_side_effects=True, vmem_limit_bytes=48 * 2**20
        ),
    )(*[pltpu.with_memory_space_constraint(x, pltpu.HBM) for x in operands])


def solution(mesh):
    nc, nt = mesh.shape["ctx"], mesh.shape["tp"]

    def local(tokens_in, w_query, w_key, w_value, grad_out, trajectory_ends):
        rows, width = tokens_in.shape
        heads = w_query.shape[1] // HD
        fits = nt == 4 and nc % 2 == 0 and heads % 2 == 0 and rows <= 512
        fits = fits and width % COLS == 0 and rows % 256 == 0
        call = functools.partial(fused_body, nc, nt) if fits else body
        return call(tokens_in, w_query, w_key, w_value, grad_out, trajectory_ends)

    return jax.shard_map(
        local,
        mesh=mesh,
        in_specs=(
            P("ctx", None),
            P(None, "tp"),
            P(None, "tp"),
            P(None, "tp"),
            P("ctx", "tp"),
            P("ctx"),
        ),
        out_specs=P(("ctx", "tp"), None),
        check_vma=False,
    )
```

```python
import functools

import jax
import jax.numpy as jnp
from jax import lax
from jax.experimental import pallas as pl
from jax.experimental.pallas import tpu as pltpu
from jax.sharding import PartitionSpec as P

HD = 128


def prefix(part, axis, combine, identity):
    count = lax.axis_size(axis)
    place = lax.axis_index(axis)
    ahead = count - 1 - place
    gathered = jax.tree.map(lambda a: lax.all_gather(a, axis), part)
    state = jax.tree.map(lambda a, e: jnp.zeros_like(a) + jnp.asarray(e, a.dtype), part, identity)

    def one(hop, state):
        source = count - 1 - hop
        return combine(
            state, jax.tree.map(lambda a: lax.dynamic_index_in_dim(a, source, 0, False), gathered)
        )

    return lax.fori_loop(0, ahead, one, state)


def joined(earlier, later):
    return (later[0] + (1.0 - later[1][0]) * earlier[0], jnp.maximum(earlier[1], later[1]))


def body(tokens_in, w_query, w_key, w_value, grad_out, trajectory_ends):
    row_count = tokens_in.shape[0]
    head_count = w_query.shape[1] // HD
    shape = (row_count, head_count, HD)
    queries = (
        jnp.dot(tokens_in, w_query, preferred_element_type=jnp.float32)
        .astype(jnp.bfloat16)
        .reshape(shape)
    )
    key_rows = (
        jnp.dot(tokens_in, w_key, preferred_element_type=jnp.float32)
        .astype(jnp.bfloat16)
        .reshape(shape)
    )
    value_rows = (
        jnp.dot(tokens_in, w_value, preferred_element_type=jnp.float32)
        .astype(jnp.bfloat16)
        .reshape(shape)
    )
    grad_rows = grad_out.reshape(shape)
    before = jnp.cumsum(trajectory_ends) - trajectory_ends
    end_total = jnp.sum(trajectory_ends)
    opened = before == 0
    closed = end_total - before == 0
    positions = jnp.arange(row_count, dtype=jnp.int32)
    pair_mask = (positions[None, :] <= positions[:, None]) & (before[:, None] == before[None, :])
    reset_any = (end_total > 0).astype(jnp.float32).reshape(1)
    open_bf = opened.astype(jnp.bfloat16)[:, None, None]
    close_bf = closed.astype(jnp.bfloat16)[:, None, None]
    carry_out = jnp.einsum(
        "shv,shk->hvk", value_rows * close_bf, key_rows, preferred_element_type=jnp.float32
    )
    grads_out = jnp.einsum(
        "thv,thk->hvk", grad_rows * open_bf, queries, preferred_element_type=jnp.float32
    )
    zero_state = jnp.zeros((head_count, HD, HD), jnp.float32)
    zero_flag = jnp.zeros((1,), jnp.float32)
    flag_list = lax.all_gather(reset_any, "ctx", axis=0, tiled=True)
    own_index = lax.axis_index("ctx")
    order = jnp.arange(flag_list.shape[0], dtype=jnp.int32)
    start_from = jnp.max(jnp.where((order < own_index) & (flag_list > 0), order, 0))
    piece = lax.all_gather(carry_out[None], "ctx", axis=0, tiled=True)
    index_list = jnp.arange(piece.shape[0], dtype=jnp.int32)
    weights = ((index_list >= start_from) & (index_list < own_index)).astype(jnp.float32)
    state_in = jnp.sum(weights[:, None, None, None] * piece, axis=0)
    grads_in = prefix((grads_out, reset_any), "ctx", joined, (zero_state, zero_flag))[0]
    scores = jnp.einsum("thv,shv->hts", grad_rows, value_rows, preferred_element_type=jnp.float32)
    scores = jnp.where(pair_mask[None], scores, 0.0).astype(jnp.bfloat16)
    attn = jnp.einsum("thk,shk->hts", queries, key_rows, preferred_element_type=jnp.float32)
    attn = jnp.where(pair_mask[None], attn, 0.0).astype(jnp.bfloat16)
    state_bf = state_in.astype(jnp.bfloat16)
    grads_bf = grads_in.astype(jnp.bfloat16)
    open_f = opened.astype(jnp.float32)[:, None, None]
    close_f = closed.astype(jnp.float32)[:, None, None]
    score_scale = 1.0 / HD
    grad_query = jnp.einsum("hts,shk->thk", scores, key_rows, preferred_element_type=jnp.float32)
    grad_query = grad_query + open_f * jnp.einsum(
        "thv,hvk->thk", grad_rows, state_bf, preferred_element_type=jnp.float32
    )
    grad_key = jnp.einsum("hts,thk->shk", scores, queries, preferred_element_type=jnp.float32)
    grad_key = grad_key + close_f * jnp.einsum(
        "shv,hvk->shk", value_rows, grads_bf, preferred_element_type=jnp.float32
    )
    grad_value = jnp.einsum("hts,thv->shv", attn, grad_rows, preferred_element_type=jnp.float32)
    grad_value = grad_value + close_f * jnp.einsum(
        "shk,hvk->shv", key_rows, grads_bf, preferred_element_type=jnp.float32
    )
    flat = (row_count, head_count * HD)
    grad_query = (score_scale * grad_query).astype(jnp.bfloat16).reshape(flat)
    grad_key = (score_scale * grad_key).astype(jnp.bfloat16).reshape(flat)
    grad_value = (score_scale * grad_value).astype(jnp.bfloat16).reshape(flat)
    dims = (((1,), (1,)), ((), ()))
    total = lax.dot_general(grad_query, w_query, dims, preferred_element_type=jnp.float32)
    total = total + lax.dot_general(grad_key, w_key, dims, preferred_element_type=jnp.float32)
    total = total + lax.dot_general(grad_value, w_value, dims, preferred_element_type=jnp.float32)
    shares = lax.psum_scatter(total, "tp", scatter_dimension=0, tiled=True)
    return shares.astype(jnp.bfloat16)


NN = ((1,), (0,))
NT = ((1,), (1,))
TN = ((0,), (0,))
COLS = 128
SPLIT = 4
BF = jnp.bfloat16
F32 = jnp.float32


def dot(a, b, dims):
    return lax.dot_general(a, b, (dims, ((), ())), preferred_element_type=F32)


def fused(
    nc, nt, tok_hbm, wq_hbm, wk_hbm, wv_hbm, g_hbm, ends_hbm, out_ref,
    ends_ref, tok, w, g, qkv, mask, flip, openc, closec, acc, dcat,
    st, fl, xfl, xr, cr, co, bs, br, fin,
    kept, sent, recd, ysent, yrecd,
    load_sem, fl_sem, x_send, x_recv, c_send, c_recv, b_send, b_recv,
    rs_send, rs_recv, y_send, y_recv,
):
    rows, width = tok.shape
    heads = g.shape[0]
    half = heads // 2
    pieces = half * SPLIT
    deep = HD // SPLIT
    chunks = width // COLS
    share = rows // nt
    ctx = lax.axis_index("ctx")
    tp = lax.axis_index("tp")
    par, pair = ctx % 2, ctx // 2
    pairs = nc // 2
    lo, hi = tp % 2, tp // 2
    mate = ctx + 1 - 2 * par
    core = tp + 1 - 2 * lo
    over = tp + 2 - 4 * hi

    turn = jnp.where(pair >= pairs // 2, 1, 0)
    token_load = pltpu.make_async_copy(tok_hbm, tok, load_sem.at[0])
    weight_loads = [
        pltpu.make_async_copy(ref, w.at[n], load_sem.at[1 + n])
        for n, ref in enumerate((wq_hbm, wk_hbm, wv_hbm))
    ]
    g_loads = [
        pltpu.make_async_copy(g_hbm.at[:, pl.ds(h * HD, HD)], g.at[h], load_sem.at[4 + h])
        for h in range(heads)
    ]
    ends_load = pltpu.make_async_copy(ends_hbm, ends_ref, load_sem.at[4 + heads])
    ends_load.start()
    token_load.start()

    @pl.when(turn == 0)
    def _():
        for n in (1, 2, 0):
            weight_loads[n].start()
        for load in g_loads:
            load.start()

    @pl.when(turn == 1)
    def _():
        weight_loads[0].start()
        for load in g_loads:
            load.start()
        for n in (1, 2):
            weight_loads[n].start()

    barrier = pltpu.get_barrier_semaphore()
    pl.semaphore_signal(barrier, inc=1, device_id={"ctx": mate}, device_id_type=pl.DeviceIdType.MESH)
    pl.semaphore_signal(barrier, inc=1, device_id={"tp": core}, device_id_type=pl.DeviceIdType.MESH)
    pl.semaphore_signal(barrier, inc=1, device_id={"tp": over}, device_id_type=pl.DeviceIdType.MESH)

    @pl.when(pair > 0)
    def _():
        pl.semaphore_signal(
            barrier, inc=1, device_id={"ctx": ctx - 2}, device_id_type=pl.DeviceIdType.MESH
        )

    @pl.when(pair < pairs - 1)
    def _():
        pl.semaphore_signal(
            barrier, inc=1, device_id={"ctx": ctx + 2}, device_id_type=pl.DeviceIdType.MESH
        )

    def remote(src, dst, send, recv, device):
        return pltpu.make_async_remote_copy(
            src_ref=src, dst_ref=dst, send_sem=send, recv_sem=recv,
            device_id=device, device_id_type=pl.DeviceIdType.MESH,
        )

    ends_load.wait()
    ends_row = jnp.broadcast_to(ends_ref[...].astype(F32), (HD, rows)).astype(BF)
    row_id = lax.broadcasted_iota(jnp.int32, (rows, rows), 0)
    col_id = lax.broadcasted_iota(jnp.int32, (rows, rows), 1)
    below = (row_id < col_id).astype(F32).astype(BF)
    above = (col_id < row_id).astype(F32).astype(BF)
    before_row = dot(ends_row, below, NN)[0:1, :]
    before_col = dot(above, ends_row, NT)
    total = jnp.sum(ends_ref[...].astype(F32), axis=1, keepdims=True)
    openc[...] = (before_col == 0.0).astype(F32)
    closec[...] = (jnp.broadcast_to(total, (rows, HD)) == before_col).astype(F32)
    fl[...] = jnp.broadcast_to((total > 0.0).astype(F32), fl.shape)
    same = before_row == jnp.broadcast_to(before_col[:, 0:1], (rows, rows))
    mask[...] = (same & (col_id <= row_id)).astype(F32).astype(BF)
    flip[...] = (same & (row_id <= col_id)).astype(F32).astype(BF)

    block = min(256, rows)
    spans = [(at, at + block) for at in range(0, rows, block)]

    def project(which):
        @pl.loop(0, rows // block)
        def _(step):
            at = pl.ds(pl.multiple_of(step * block, block), block)
            made = dot(tok[at, :], w[which], NN).astype(BF)
            for h in range(heads):
                qkv[which, h, at, :] = made[:, h * HD : (h + 1) * HD]

    def x_copy(d, i):
        return remote(
            st.at[d, (1 - par) * pieces + i], xr.at[d, i],
            x_send.at[d, i], x_recv.at[d, i], {"ctx": mate},
        )

    def state(d, h):
        if d == 0:
            made = dot(qkv[2, h] * closec[...].astype(BF), qkv[1, h], TN)
        else:
            made = dot(g[h] * openc[...].astype(BF), qkv[0, h], TN)
        for n in range(SPLIT):
            st[d, h * SPLIT + n] = made[n * deep : (n + 1) * deep]

    def give(d):
        for i in range(half):
            state(d, (1 - par) * half + i)
            for n in range(SPLIT):
                x_copy(d, i * SPLIT + n).start()

    def keys_values():
        for n in (1, 2):
            weight_loads[n].wait()
            project(n)

    def queries():
        weight_loads[0].wait()
        project(0)

    token_load.wait()

    @pl.when(turn == 0)
    def _():
        keys_values()

    @pl.when(turn == 1)
    def _():
        queries()

    for load in g_loads:
        load.wait()
    waits = 3 + jnp.where(pair > 0, 1, 0) + jnp.where(pair < pairs - 1, 1, 0)
    pl.semaphore_wait(barrier, waits)
    flag_copy = remote(fl, xfl, fl_sem.at[0], fl_sem.at[1], {"ctx": mate})
    flag_copy.start()

    @pl.when(turn == 0)
    def _():
        give(0)
        queries()
        give(1)

    @pl.when(turn == 1)
    def _():
        give(1)
        keys_values()
        give(0)

    for i in range(half):
        state(0, par * half + i)
        state(1, par * half + i)

    def within(h):
        for start, stop in spans:
            at, upto, onward = slice(start, stop), slice(0, stop), slice(start, rows)
            scores = dot(g[h, at, :], qkv[2, h, upto, :], NT).astype(BF) * mask[at, upto]
            acc[0, h, at, :] = dot(scores, qkv[1, h, upto, :], NN)
            turned = dot(qkv[2, h, at, :], g[h, onward, :], NT).astype(BF) * flip[at, onward]
            acc[1, h, at, :] = dot(turned, qkv[0, h, onward, :], NN)
            attn = dot(qkv[1, h, at, :], qkv[0, h, onward, :], NT).astype(BF) * flip[at, onward]
            acc[2, h, at, :] = dot(attn, g[h, onward, :], NN)

    def within_some(first, last):
        @pl.loop(first, last)
        def _(h):
            within(h)

    def c_copy(d, i):
        return remote(
            co.at[d, i], cr.at[d, i], c_send.at[d, i], c_recv.at[d, i],
            {"ctx": ctx + 2 - 4 * d},
        )

    def b_copy(d, i):
        return remote(bs.at[d, i], br.at[d, i], b_send.at[d, i], b_recv.at[d, i], {"ctx": mate})

    def has_next(d):
        return ((d == 0) & (pair < pairs - 1)) | ((d == 1) & (pair > 0))

    def has_prev(d):
        return ((d == 0) & (pair > 0)) | ((d == 1) & (pair < pairs - 1))

    def place(i):
        return slice(i % SPLIT * deep, (i % SPLIT + 1) * deep)

    def carry(d):
        first_here = par == d
        more, begun = has_next(d), has_prev(d)
        own_flag, mate_flag = fl[0:1, :], xfl[0:1, :]
        first_flag = jnp.where(first_here, own_flag, mate_flag)
        second_flag = jnp.where(first_here, mate_flag, own_flag)

        @pl.when(jnp.logical_not(begun))
        def _():
            cr[d] = jnp.zeros(cr.shape[1:], F32)

        for i in range(pieces):
            x_copy(d, i).wait_recv()
            own, other = st[d, par * pieces + i], xr[d, i]
            first = jnp.where(first_here, own, other)
            second = jnp.where(first_here, other, own)

            @pl.when(begun)
            def _():
                c_copy(d, i).wait_recv()

            into = cr[d, i]
            inner = first + (1.0 - first_flag) * into

            @pl.when(more)
            def _():
                co[d, i] = second + (1.0 - second_flag) * inner
                c_copy(d, i).start()

            bs[d, i] = jnp.where(first_here, inner, into)
            b_copy(d, i).start()
            mine = jnp.where(first_here, into, inner).astype(BF)
            fin[d, par * half + i // SPLIT, place(i), :] = mine

    scale = 1.0 / HD

    def finish(d, h):
        at = pl.ds(pl.multiple_of(h * HD, HD), HD)

        @pl.when(d == 0)
        def _():
            dq = acc[0, h] + openc[...] * dot(g[h], fin[0, h], NN)
            dcat[0, :, at] = (scale * dq).astype(BF)

        @pl.when(d == 1)
        def _():
            b_in, closed = fin[1, h], closec[...]
            dk = acc[1, h] + closed * dot(qkv[2, h], b_in, NN)
            dv = acc[2, h] + closed * dot(qkv[1, h], b_in, NT)
            dcat[1, :, at] = (scale * dk).astype(BF)
            dcat[2, :, at] = (scale * dv).astype(BF)

    def finish_own(d):
        @pl.loop(0, half)
        def _(i):
            finish(d, par * half + i)

    def finish_mate(d):
        @pl.loop(0, half)
        def _(i):
            h = (1 - par) * half + i
            for n in range(SPLIT):
                b_copy(d, i * SPLIT + n).wait_recv()
                fin[d, h, place(n), :] = br[d, i * SPLIT + n].astype(BF)
            finish(d, h)

    at_end = (pair == 0) | (pair == pairs - 1)
    early = jnp.where(at_end, 0, heads // 4)
    late = jnp.where(at_end, heads, heads // 2)
    flag_copy.wait_recv()
    within_some(0, early)
    carry(turn)
    within_some(early, late)

    @pl.when(at_end)
    def _():
        finish_own(turn)
        finish_mate(turn)

    carry(1 - turn)
    within_some(late, heads)

    @pl.when(jnp.logical_not(at_end))
    def _():
        finish_own(turn)
        finish_mate(turn)

    finish_own(1 - turn)
    finish_mate(1 - turn)

    def rs_copy(part, j):
        return remote(
            sent.at[part, j], recd.at[part, j], rs_send.at[part, j], rs_recv.at[part, j],
            {"tp": core},
        )

    def y_copy(j):
        return remote(ysent.at[j], yrecd.at[j], y_send.at[j], y_recv.at[j], {"tp": over})

    def product(part, j):
        side = jnp.where(part == 0, 1 - hi, hi)
        at = pl.ds(pl.multiple_of(side * 2 * share, 2 * share), 2 * share)
        cols = pl.ds(pl.multiple_of(j * COLS, COLS), COLS)
        made = dot(dcat[0, at, :], w[0, cols, :], NT)
        made = made + dot(dcat[1, at, :], w[1, cols, :], NT)
        made = made + dot(dcat[2, at, :], w[2, cols, :], NT)
        low, high = made[0:share], made[share : 2 * share]
        sent[part, j] = jnp.where(lo == 0, high, low)
        kept[part, j] = jnp.where(lo == 0, low, high)
        rs_copy(part, j).start()

    def pass_on(j):
        rs_copy(0, j).wait_recv()
        ysent[j] = kept[0, j] + recd[0, j]
        y_copy(j).start()

    product(0, 0)

    @pl.loop(1, chunks)
    def _(j):
        product(0, j)
        pass_on(j - 1)

    product(1, 0)
    pass_on(chunks - 1)

    @pl.loop(1, chunks)
    def _(j):
        product(1, j)

    for j in range(chunks):
        rs_copy(1, j).wait_recv()
        y_copy(j).wait_recv()
        out_ref[:, j * COLS : (j + 1) * COLS] = (kept[1, j] + recd[1, j] + yrecd[j]).astype(BF)

    flag_copy.wait_send()
    for d in range(2):
        for i in range(pieces):
            x_copy(d, i).wait_send()
            b_copy(d, i).wait_send()

        @pl.when(has_next(d))
        def _():
            for i in range(pieces):
                c_copy(d, i).wait_send()

    @pl.loop(0, chunks)
    def _(j):
        rs_copy(0, j).wait_send()
        rs_copy(1, j).wait_send()
        y_copy(j).wait_send()


def fused_body(nc, nt, tokens_in, w_query, w_key, w_value, grad_out, trajectory_ends):
    rows, width = tokens_in.shape
    inner = w_query.shape[1]
    heads = inner // HD
    half = heads // 2
    share = rows // nt
    chunks = width // COLS
    outside = pl.BlockSpec(memory_space=pltpu.HBM)
    vmem = pl.BlockSpec(memory_space=pltpu.VMEM)
    dma = pltpu.SemaphoreType.DMA
    pieces = half * SPLIT
    deep = HD // SPLIT
    states = pltpu.VMEM((2, pieces, deep, HD), F32)
    piece = (chunks, share, COLS)
    operands = (tokens_in, w_query, w_key, w_value, grad_out, trajectory_ends.reshape(1, rows))
    return pl.pallas_call(
        functools.partial(fused, nc, nt),
        out_shape=jax.ShapeDtypeStruct((share, width), BF),
        in_specs=[outside] * 6,
        out_specs=vmem,
        scratch_shapes=[
            pltpu.VMEM((1, rows), jnp.int32),
            pltpu.VMEM((rows, width), BF),
            pltpu.VMEM((3, width, inner), BF),
            pltpu.VMEM((heads, rows, HD), BF),
            pltpu.VMEM((3, heads, rows, HD), BF),
            pltpu.VMEM((rows, rows), BF),
            pltpu.VMEM((rows, rows), BF),
            pltpu.VMEM((rows, HD), F32),
            pltpu.VMEM((rows, HD), F32),
            pltpu.VMEM((3, heads, rows, HD), F32),
            pltpu.VMEM((3, rows, inner), BF),
            pltpu.VMEM((2, heads * SPLIT, deep, HD), F32),
            pltpu.VMEM((8, HD), F32),
            pltpu.VMEM((8, HD), F32),
            states, states, states, states, states,
            pltpu.VMEM((2, heads, HD, HD), BF),
            pltpu.VMEM((2, *piece), F32),
            pltpu.VMEM((2, *piece), F32),
            pltpu.VMEM((2, *piece), F32),
            pltpu.VMEM(piece, F32),
            pltpu.VMEM(piece, F32),
            dma((5 + heads,)),
            dma((2,)),
            dma((2, pieces)), dma((2, pieces)),
            dma((2, pieces)), dma((2, pieces)),
            dma((2, pieces)), dma((2, pieces)),
            dma((2, chunks)), dma((2, chunks)),
            dma((chunks,)), dma((chunks,)),
        ],
        compiler_params=pltpu.CompilerParams(
            collective_id=0, has_side_effects=True, vmem_limit_bytes=48 * 2**20
        ),
    )(*[pltpu.with_memory_space_constraint(x, pltpu.HBM) for x in operands])


def solution(mesh):
    nc, nt = mesh.shape["ctx"], mesh.shape["tp"]

    def local(tokens_in, w_query, w_key, w_value, grad_out, trajectory_ends):
        rows, width = tokens_in.shape
        heads = w_query.shape[1] // HD
        fits = nt == 4 and nc % 2 == 0 and heads % 2 == 0 and rows <= 512
        fits = fits and width % COLS == 0 and rows % 256 == 0
        call = functools.partial(fused_body, nc, nt) if fits else body
        return call(tokens_in, w_query, w_key, w_value, grad_out, trajectory_ends)

    return jax.shard_map(
        local,
        mesh=mesh,
        in_specs=(
            P("ctx", None),
            P(None, "tp"),
            P(None, "tp"),
            P(None, "tp"),
            P("ctx", "tp"),
            P("ctx"),
        ),
        out_specs=P(("ctx", "tp"), None),
        check_vma=False,
    )
```
